256 devices in a mesh: row: 8 (over y_hi, x), col: 16 (over y_lo, z), rep: 2 (over core).
Axes of the slice: x: 4, y: 4 (y_hi: 2, y_lo: 2; y = y_hi * 2 + y_lo), z: 8, core: 2. Of those that a mesh axis runs over, the one named last changes fastest.
Arguments:
- inputs: bfloat16 [2048, 12288], P(('rep', 'col'), 'row'), parts along dimension 0, may hold values from -30 to 30
- w_qkv: bfloat16 [12288, 18432], P('row', 'col'), may hold values from -1 to 1
- out_grad: bfloat16 [2048, 6144], P(('rep', 'row'), 'col'), parts along dimension 0, may hold values from -6 to 6
Outputs:
- attended: bfloat16 [2048, 6144], P(('rep', 'row'), 'col'), parts along dimension 0
- input_grad: bfloat16 [2048, 12288], P(('rep', 'col'), 'row'), parts along dimension 0
- weight_grad: bfloat16 [24576, 18432], P(('rep', 'row'), 'col'), parts along dimension 0
The draws below stay inside these ranges and needn't reach their ends.
There are 2 independent parts, one for each index of `rep`. The reference program is written for one: setup_inputs(seed, part) draws one part's arguments, and reference() takes and returns one part's arrays. A program takes and returns all parts, laid end to end along the dimension named above; an argument that names none is the same for every part. Nothing has to cross between parts.
All inputs are finite; a program needn't handle non-finite values.
Results may differ from the reference program's by a relative error of at most 0.02.
Values may be sent and summed in bfloat16 or wider, within the bound.
No kernel may reach another device: no remote copies, remote signals or barrier semaphores. Data moves between devices by JAX's collectives and lax.ppermute only.
A program may use at most 64 MiB of HBM per device.

```python
import math
import jax
import jax.numpy as jnp
from jax import lax

D = 12288
HEADS = 48
HD = 128
SEQ = 1024
FQKV = 18432
ATT = 6144


def draw_inputs(key, part):
    key = jax.random.fold_in(key, 3)
    first_key = jax.random.fold_in(key, 0)
    values = jnp.clip(jax.random.normal(first_key, (SEQ, D), jnp.float32), -6.0, 6.0)
    return values.astype(jnp.bfloat16)


def draw_w_qkv(key, part):
    key = jax.random.fold_in(key, 7)
    first_key = jax.random.fold_in(key, 0)
    normal_part = jnp.clip(jax.random.normal(first_key, (D, HEADS, 3, HD), jnp.float32), -4.0, 4.0) / math.sqrt(D)
    return normal_part.reshape(D, HEADS * 3 * HD).astype(jnp.bfloat16)


def levels(key, shape, pieces, least, largest):
    def one(dim, shards_of):
        draws = jax.random.uniform(jax.random.fold_in(jax.random.fold_in(key, 6), dim), (shards_of,), jnp.float32, least / len(pieces), largest / len(pieces))
        return jnp.repeat(jnp.exp(draws), shape[dim] // shards_of).reshape((-1,) + (1,) * (len(shape) - dim - 1))

    loudness = one(*pieces[0])
    for cut in pieces[1:]:
        loudness = loudness * one(*cut)
    return loudness


def scatter_about(rng, shape, spread, most, pieces=(), kind=jnp.bfloat16):
    entries = jax.random.normal(rng, shape, jnp.float32) * spread
    if len(pieces) > 0:
        entries = levels(rng, shape, pieces, -0.22, 0.18) * entries
    return jnp.clip(entries, min=-most, max=most).astype(kind)


def setup_inputs(seed: int = 0, part: int = 0) -> dict:
    key_list = jax.random.split(jax.random.key(seed), 4)
    own_keys = jax.random.split(jax.random.fold_in(key_list[3], part), 4)
    inputs = draw_inputs(jax.random.fold_in(jax.random.fold_in(key_list[3], part), 71), part)
    w_qkv = draw_w_qkv(jax.random.fold_in(key_list[3], 71), part)
    out_grad = scatter_about(own_keys[2], (SEQ, ATT), 1.0, 6.0, ((0, 8), (1, 16)))
    return dict(inputs=inputs, w_qkv=w_qkv, out_grad=out_grad)


def head_pass(packed):
    q_head, k_head, v_head, g_head = packed
    inv_root = 1.0 / math.sqrt(HD)
    scores = jnp.dot(q_head, k_head.T, preferred_element_type=jnp.float32) * inv_root
    positions = jnp.arange(SEQ, dtype=jnp.int32)
    visible = positions[None, :] <= positions[:, None]
    scores = jnp.where(visible, scores, jnp.float32(-1e+30))
    maxima = lax.optimization_barrier(jnp.max(scores, axis=-1))
    log_total = maxima + jnp.log(lax.optimization_barrier(jnp.sum(jnp.exp(scores - maxima[:, None]), axis=-1)))
    attn_probs = jnp.exp(scores - log_total[:, None]).astype(jnp.bfloat16)
    attended = jnp.dot(attn_probs, v_head, preferred_element_type=jnp.float32).astype(jnp.bfloat16)
    row_dots = lax.optimization_barrier(jnp.sum(g_head.astype(jnp.float32) * attended.astype(jnp.float32), axis=-1))
    dprobs = jnp.dot(g_head, v_head.T, preferred_element_type=jnp.float32)
    dscores = (attn_probs.astype(jnp.float32) * (dprobs - row_dots[:, None])).astype(jnp.bfloat16)
    q_grad = jnp.dot(dscores, k_head, preferred_element_type=jnp.float32) * inv_root
    k_grad = jnp.dot(dscores.T, q_head, preferred_element_type=jnp.float32) * inv_root
    v_grad = jnp.dot(attn_probs.T, g_head, preferred_element_type=jnp.float32)
    return (attended, jnp.stack([q_grad, k_grad, v_grad], axis=1).astype(jnp.bfloat16))

def reference(inputs, w_qkv, out_grad):
    qkv = jnp.dot(inputs, w_qkv, preferred_element_type=jnp.float32).astype(jnp.bfloat16)
    qkv = qkv.reshape(SEQ, HEADS, 3, HD).transpose(1, 2, 0, 3)
    g_heads = out_grad.reshape(SEQ, HEADS, HD).transpose(1, 0, 2)
    attended, qkv_grad = lax.map(head_pass, (qkv[:, 0], qkv[:, 1], qkv[:, 2], g_heads))
    attended = attended.transpose(1, 0, 2).reshape(SEQ, HEADS * HD)
    qkv_grad = qkv_grad.transpose(1, 0, 2, 3).reshape(SEQ, FQKV)
    weight_grad = lax.dot_general(inputs, qkv_grad, (((0,), (0,)), ((), ())), preferred_element_type=jnp.float32).astype(jnp.bfloat16)
    input_grad = lax.dot_general(qkv_grad, w_qkv, (((1,), (1,)), ((), ())), preferred_element_type=jnp.float32).astype(jnp.bfloat16)
    return (attended, input_grad, weight_grad)
```

```python
import functools
import math

import jax
import jax.numpy as jnp
from jax import lax
from jax.experimental import pallas as pl
from jax.experimental.pallas import tpu as pltpu
from jax.sharding import PartitionSpec as P

HD = 128
QB = 256
F32 = jnp.float32
BF16 = jnp.bfloat16


def project_kernel(units, unit_rows, first_row, aliased, *refs):
    xs, w = refs[:units], refs[units]
    out, x_all, x, sem = refs[units + 1 + aliased :]
    for j in range(units):
        x[j * unit_rows : (j + 1) * unit_rows] = xs[j][...]
    copy = pltpu.make_async_copy(x, x_all.at[pl.ds(first_row, units * unit_rows)], sem)
    copy.start()
    step = 3 * HD
    for n in range(0, out.shape[1], step):
        cols = slice(n, n + step)
        out[:, cols] = jnp.dot(x[...], w[:, cols], preferred_element_type=F32).astype(BF16)
    copy.wait()


def project(xs, w_qkv, seq, first_row, x_all=None):
    units, (unit_rows, depth), width = len(xs), xs[0].shape, w_qkv.shape[1]
    any_spec = pl.BlockSpec(memory_space=pl.ANY)
    vmem = pl.BlockSpec(memory_space=pltpu.VMEM)
    aliased = x_all is not None
    return pl.pallas_call(
        functools.partial(project_kernel, units, unit_rows, first_row, aliased),
        out_shape=(
            jax.ShapeDtypeStruct((units * unit_rows, width), BF16),
            jax.ShapeDtypeStruct((seq, depth), BF16),
        ),
        in_specs=[vmem] * (units + 1) + [any_spec] * aliased,
        out_specs=(vmem, any_spec),
        scratch_shapes=[pltpu.VMEM((units * unit_rows, depth), BF16), pltpu.SemaphoreType.DMA],
        input_output_aliases={units + 1: 1} if aliased else {},
        compiler_params=pltpu.CompilerParams(vmem_limit_bytes=24 * 1024 * 1024),
        cost_estimate=pl.CostEstimate(
            flops=2 * units * unit_rows * depth * width,
            bytes_accessed=2 * (depth * width + units * unit_rows * (2 * depth + width)),
            transcendentals=0,
        ),
    )(*xs, w_qkv, *([x_all] if aliased else []))


def sum_kernel(got, out):
    total = got[0].astype(F32)
    for i in range(1, got.shape[0]):
        total = total + got[i].astype(F32)
    total = total.astype(BF16)
    for i in range(got.shape[0]):
        out[i] = total


def sum_and_spread(got):
    return pl.pallas_call(
        sum_kernel,
        out_shape=jax.ShapeDtypeStruct(got.shape, BF16),
        cost_estimate=pl.CostEstimate(
            flops=got.size, bytes_accessed=4 * got.size, transcendentals=0
        ),
    )(got)


def attention_kernel(heads, units, unit_rows, place_ref, *refs):
    *chunks, og_ref, att_out, grad_out = refs[:-8]
    qkv, og, att, grad, dk_acc, dv_acc, in_sem, out_sem = refs[-8:]
    per_chunk = units // len(chunks)
    seq = units * unit_rows
    copies = [
        pltpu.make_async_copy(
            chunks[j // per_chunk].at[pl.ds(j % per_chunk * unit_rows, unit_rows)],
            qkv.at[pl.ds(pl.multiple_of(place_ref[j], unit_rows), unit_rows)],
            in_sem.at[j],
        )
        for j in range(units)
    ]
    copies.append(
        pltpu.make_async_copy(og_ref.at[:, pl.ds(0, heads * HD)], og, in_sem.at[units])
    )
    for c in copies:
        c.start()
    for c in copies:
        c.wait()
    inv_root = 1.0 / math.sqrt(HD)
    to_base2 = inv_root * math.log2(math.e)
    nt = (((1,), (1,)), ((), ()))
    nn = (((1,), (0,)), ((), ()))

    def dot(a, b, dims):
        return lax.dot_general(a, b, dims, preferred_element_type=F32)

    for h in range(heads):
        base = h * 3 * HD
        k_t = qkv[:, base + HD : base + 2 * HD].T
        v_t = qkv[:, base + 2 * HD : base + 3 * HD].T
        for i in reversed(range(seq // QB)):
            rows = slice(i * QB, (i + 1) * QB)
            n_keys = (i + 1) * QB
            keys = slice(0, n_keys)
            q = qkv[rows, base : base + HD]
            k = qkv[keys, base + HD : base + 2 * HD]
            v = qkv[keys, base + 2 * HD : base + 3 * HD]
            g = og[rows, h * HD : (h + 1) * HD]
            scores = dot(k, q, nt) * to_base2
            key_pos = lax.broadcasted_iota(jnp.int32, (n_keys, QB), 0)
            query_pos = i * QB + lax.broadcasted_iota(jnp.int32, (n_keys, QB), 1)
            scores = jnp.where(key_pos <= query_pos, scores, F32(-1e30))
            top = jnp.max(scores, axis=0, keepdims=True)
            expo = jnp.exp2(scores - top)
            total = jnp.sum(expo, axis=0, keepdims=True)
            probs = expo * (1.0 / total)
            probs16 = probs.astype(BF16)
            attended_t = dot(v_t[:, keys], probs16, nn).astype(BF16)
            dots = jnp.sum(g.T.astype(F32) * attended_t.astype(F32), axis=0, keepdims=True)
            att[rows, h * HD : (h + 1) * HD] = attended_t.T
            dscores = (probs * (dot(v, g, nt) - dots)).astype(BF16)
            dq_t = dot(k_t[:, keys], dscores, nn) * inv_root
            grad[rows, base : base + HD] = dq_t.astype(BF16).T
            dk = dot(dscores, q, nn)
            dv = dot(probs16, g, nn)
            if n_keys == seq:
                dk_acc[...] = dk
                dv_acc[...] = dv
            else:
                dk_acc[keys] += dk
                dv_acc[keys] += dv
        grad[:, base + HD : base + 2 * HD] = (dk_acc[...] * inv_root).astype(BF16)
        grad[:, base + 2 * HD : base + 3 * HD] = dv_acc[...].astype(BF16)

    out_rows = att_out.shape[0]
    outs = [
        pltpu.make_async_copy(
            att.at[pl.ds(pl.multiple_of(place_ref[units], out_rows), out_rows)],
            att_out,
            out_sem.at[units],
        )
    ]
    for j in range(units):
        outs.append(
            pltpu.make_async_copy(
                grad.at[pl.ds(pl.multiple_of(place_ref[j], unit_rows), unit_rows)],
                grad_out.at[pl.ds(j * unit_rows, unit_rows)],
                out_sem.at[j],
            )
        )
    for c in outs:
        c.start()
    for c in outs:
        c.wait()


def attention(places, unit_rows, chunks, og_full, own_rows):
    width = chunks[0].shape[1]
    seq = sum(c.shape[0] for c in chunks)
    units = seq // unit_rows
    heads = width // (3 * HD)
    any_spec = pl.BlockSpec(memory_space=pl.ANY)
    return pl.pallas_call(
        functools.partial(attention_kernel, heads, units, unit_rows),
        out_shape=(
            jax.ShapeDtypeStruct((own_rows, heads * HD), BF16),
            jax.ShapeDtypeStruct((seq, width), BF16),
        ),
        in_specs=[pl.BlockSpec(memory_space=pltpu.SMEM)] + [any_spec] * (len(chunks) + 1),
        out_specs=(any_spec, any_spec),
        scratch_shapes=[
            pltpu.VMEM((seq, width), BF16),
            pltpu.VMEM((seq, heads * HD), BF16),
            pltpu.VMEM((seq, heads * HD), BF16),
            pltpu.VMEM((seq, width), BF16),
            pltpu.VMEM((seq, HD), F32),
            pltpu.VMEM((seq, HD), F32),
            pltpu.SemaphoreType.DMA((units + 1,)),
            pltpu.SemaphoreType.DMA((units + 1,)),
        ],
        compiler_params=pltpu.CompilerParams(vmem_limit_bytes=40 * 1024 * 1024),
        cost_estimate=pl.CostEstimate(
            flops=12 * heads * seq * seq * HD * 5 // 8,
            bytes_accessed=2 * seq * (width * 2 + heads * HD * 2),
            transcendentals=heads * seq * seq * 5 // 8,
        ),
    )(places, *chunks, og_full)


def per_device(inputs, w_qkv, out_grad):
    tok = inputs.shape[0]
    own_rows = out_grad.shape[0]
    rows = lax.axis_size("row")
    cols = lax.axis_size("col")
    nz = cols // 2
    seq = cols * tok
    row = lax.axis_index("row")
    col = lax.axis_index("col")
    z, y_own = col % nz, col // nz

    def along_z(step):
        return [(y * nz + a, y * nz + (a + step) % nz) for y in range(2) for a in range(nz)]

    def up(v):
        return lax.ppermute(v, "col", along_z(1))

    def down(v):
        return lax.ppermute(v, "col", along_z(-1))

    def swap_y(v):
        return lax.ppermute(v, "col", [(c, (c + nz) % cols) for c in range(cols)])

    def over_rows(partial):
        shape = (rows, partial.shape[0] // rows, partial.shape[1])
        got = lax.all_to_all(partial.reshape(shape), "row", 0, 0, tiled=True)
        spread = lax.all_to_all(sum_and_spread(got), "row", 0, 0, tiled=True)
        return spread.reshape(partial.shape)

    og_full = lax.all_gather(
        jnp.concatenate([out_grad, out_grad], axis=1), "row", axis=0, tiled=True
    )

    a0 = inputs
    c0 = swap_y(inputs)
    af1, ab1 = up(a0), down(a0)
    cf1, cb1 = up(c0), down(c0)
    af2, ab2 = up(af1), down(ab1)
    cf2, cb2 = up(cf1), down(cb1)
    af3, ab3 = up(af2), down(ab2)
    cf3, cb3 = up(cf2), down(cb2)
    a4, c4 = up(af3), down(cb3)
    shifts = [0, -1, 1, -2, 2, -3, 3, 4]
    unit_place = [
        (y_own ^ u) * (nz * tok) + ((z + d + nz) % nz) * tok for d in shifts for u in range(2)
    ]
    places = jnp.stack(unit_place + [row * own_rows]).astype(jnp.int32)

    part, x_all = project([a0, c0, af1, cf1, ab1, cb1, af2, cf2], w_qkv, seq, 0)
    first = over_rows(part)
    part, x_all = project([ab2, cb2, af3, cf3, ab3, cb3, a4, c4], w_qkv, seq, seq // 2, x_all)
    second = over_rows(part)

    attended, grads = attention(places, tok, [first, second], og_full, own_rows)

    def back(lo, hi):
        return lax.dot_general(
            grads[lo * tok : hi * tok],
            w_qkv,
            (((1,), (1,)), ((), ())),
            preferred_element_type=F32,
        ).astype(BF16)

    g_far, g_near = back(10, 16), back(0, 10)

    def part_of(unit):
        if unit >= 10:
            return g_far[(unit - 10) * tok : (unit - 9) * tok]
        return g_near[unit * tok : (unit + 1) * tok]

    def add(*parts):
        return sum(p.astype(F32) for p in parts).astype(BF16)

    au, cd = up(part_of(14)), down(part_of(15))
    c_up = up(part_of(13))
    c_down = down(add(part_of(11), cd))
    a_up = up(add(part_of(12), au))
    a_down = down(part_of(10))
    c_up, c_down = up(add(part_of(9), c_up)), down(add(part_of(7), c_down))
    a_up, a_down = up(add(part_of(8), a_up)), down(add(part_of(6), a_down))
    c_up, c_down = up(add(part_of(5), c_up)), down(add(part_of(3), c_down))
    a_up, a_down = up(add(part_of(4), a_up)), down(add(part_of(2), a_down))
    other = swap_y(add(part_of(1), c_up, c_down))
    input_grad = add(part_of(0), a_up, a_down, other)

    weight_grad = lax.dot_general(
        x_all, grads, (((0,), (0,)), ((), ())), preferred_element_type=F32
    ).astype(BF16)
    return attended, input_grad, weight_grad


def solution(mesh):
    placed = (P(("rep", "col"), "row"), P("row", "col"), P(("rep", "row"), "col"))
    return jax.shard_map(
        per_device,
        mesh=mesh,
        in_specs=placed,
        out_specs=(P(("rep", "row"), "col"), P(("rep", "col"), "row"), P(("rep", "row"), "col")),
        check_vma=False,
    )
```

```python
import functools
import math

import jax
import jax.numpy as jnp
from jax import lax
from jax.experimental import pallas as pl
from jax.experimental.pallas import tpu as pltpu
from jax.sharding import PartitionSpec as P

HD = 128
QB = 512
F32 = jnp.float32
BF16 = jnp.bfloat16


def hold_kernel(w_hbm, w, sem):
    step = w.shape[0] // sem.shape[0]
    copies = [
        pltpu.make_async_copy(w_hbm.at[pl.ds(i * step, step)], w.at[pl.ds(i * step, step)], sem.at[i])
        for i in range(sem.shape[0])
    ]
    for c in copies:
        c.start()
    for c in copies:
        c.wait()


def hold(w_qkv):
    return pl.pallas_call(
        hold_kernel,
        out_shape=pltpu.VMEM(w_qkv.shape, BF16),
        in_specs=[pl.BlockSpec(memory_space=pltpu.HBM)],
        out_specs=pl.BlockSpec(memory_space=pltpu.VMEM),
        scratch_shapes=[pltpu.SemaphoreType.DMA((8,))],
    )(w_qkv)


def project_kernel(units, unit_rows, first_row, others, *refs):
    xs, w = refs[:units], refs[units]
    outs, x_all = refs[units + 1 + others : -6], refs[-6]
    x, y, in_sem, lay_sem, out_sem = refs[-5:]
    nx = units // 2
    me = lax.rem(lax.axis_index("row"), nx)
    slots = [2 * lax.rem(j // 2 + nx - me, nx) + j % 2 for j in range(units)]
    slots = [pl.multiple_of(slot * unit_rows, unit_rows) for slot in slots]

    def in_copy(j):
        return pltpu.make_async_copy(xs[j], x.at[pl.ds(slots[j], unit_rows)], in_sem.at[j])

    lays = [
        pltpu.make_async_copy(
            x.at[pl.ds(slots[j], unit_rows)],
            x_all.at[pl.ds(first_row + j * unit_rows, unit_rows)],
            lay_sem.at[j],
        )
        for j in range(units)
    ]
    for j in range(units):
        in_copy(j).start()
    for j in range(units):
        in_copy(j).wait()
    for c in lays:
        c.start()
    tile = 3 * HD
    rows = outs[0].shape[0]
    places = [0, rows, 3 * rows, 2 * rows, 2 * rows + rows // 2]
    sends = []
    for n in range(w.shape[1] // tile):
        cols = slice(n * tile, (n + 1) * tile)
        y[:, cols] = jnp.dot(x[...], w[:, cols], preferred_element_type=F32).astype(BF16)
        for i, out in enumerate(outs):
            src = y.at[pl.ds(places[i], out.shape[0]), pl.ds(n * tile, tile)]
            sends.append(
                pltpu.make_async_copy(src, out.at[:, pl.ds(n * tile, tile)], out_sem.at[n, i])
            )
            sends[-1].start()
    for c in lays + sends:
        c.wait()


def project(xs, w_vmem, seq, first_row, x_all=None, after=()):
    units, (unit_rows, depth), width = len(xs), xs[0].shape, w_vmem.shape[1]
    hbm = pl.BlockSpec(memory_space=pltpu.HBM)
    others = ([] if x_all is None else [x_all]) + list(after)
    quarter = pltpu.HBM((units * unit_rows // 4, width), BF16)
    half = pltpu.HBM((units * unit_rows // 8, width), BF16)
    xs = [pltpu.with_memory_space_constraint(v, pltpu.HBM) for v in xs]
    *parts, x_all = pl.pallas_call(
        functools.partial(project_kernel, units, unit_rows, first_row, len(others)),
        out_shape=[quarter] * 3 + [half] * 2 + [pltpu.HBM((seq, depth), BF16)],
        in_specs=[hbm] * units + [pl.BlockSpec(memory_space=pltpu.VMEM)] + [hbm] * len(others),
        out_specs=[hbm] * 6,
        scratch_shapes=[
            pltpu.VMEM((units * unit_rows, depth), BF16),
            pltpu.VMEM((units * unit_rows, width), BF16),
            pltpu.SemaphoreType.DMA((units,)),
            pltpu.SemaphoreType.DMA((units,)),
            pltpu.SemaphoreType.DMA((width // (3 * HD), 5)),
        ],
        input_output_aliases={} if x_all is None else {units + 1: 5},
        compiler_params=pltpu.CompilerParams(vmem_limit_bytes=24 * 1024 * 1024),
        cost_estimate=pl.CostEstimate(
            flops=2 * units * unit_rows * depth * width,
            bytes_accessed=2 * units * unit_rows * (2 * depth + width),
            transcendentals=0,
        ),
    )(*xs, w_vmem, *others)
    return parts, x_all


def add_half_kernel(which, whole, half, out):
    @pl.when(pl.program_id(0) == which)
    def _():
        out[...] = (whole[...].astype(F32) + half[...].astype(F32)).astype(BF16)

    @pl.when(pl.program_id(0) != which)
    def _():
        out[...] = whole[...]


def add_half(whole, half, which):
    return pl.pallas_call(
        functools.partial(add_half_kernel, which),
        grid=(2,),
        out_shape=jax.ShapeDtypeStruct(whole.shape, BF16),
        in_specs=[by_rows(whole), pl.BlockSpec(half.shape, lambda i: (0, 0))],
        out_specs=by_rows(whole),
    )(whole, half)


def sum_beside_kernel(count, *refs):
    total = refs[0][...].astype(F32)
    for r in refs[1:count]:
        total = total + r[...].astype(F32)
    width = total.shape[1]
    out = refs[-1]
    out[:, :width] = total.astype(BF16)
    out[:, width:] = refs[count][...]


def by_rows(array, steps=2):
    rows, width = array.shape
    return pl.BlockSpec((rows // steps, width), lambda i: (i, 0))


def sum_beside(parts, beside):
    rows, width = parts[0].shape
    out = jax.ShapeDtypeStruct((rows, width + beside.shape[1]), BF16)
    return pl.pallas_call(
        functools.partial(sum_beside_kernel, len(parts)),
        grid=(2,),
        out_shape=out,
        in_specs=[by_rows(p) for p in (*parts, beside)],
        out_specs=by_rows(out),
    )(*parts, beside)


def merge_kernel(width, mine, got, out):
    total = mine[:, :width].astype(F32) + got[:, :width].astype(F32)
    out[:, :width] = total.astype(BF16)
    out[:, width : mine.shape[1]] = mine[:, width:]
    out[:, mine.shape[1] :] = got[:, width:]


def merge(mine, got, width):
    rows, both = mine.shape
    out = jax.ShapeDtypeStruct((rows, 2 * both - width), BF16)
    return pl.pallas_call(
        functools.partial(merge_kernel, width),
        grid=(2,),
        out_shape=out,
        in_specs=[by_rows(mine), by_rows(got)],
        out_specs=by_rows(out),
    )(mine, got)


def attention_kernel(heads, order, unit_rows, *refs):
    pieces, (w_hbm, att_out, grad_out) = refs[:10], refs[10:13]
    g_outs = refs[13 : 13 + len(order)]
    qkv, og, att, grad, dk_acc, dv_acc, w, in_sem, w_sem, out_sem = refs[13 + len(order) :]
    seq, width = qkv.shape
    out_rows = att_out.shape[0]
    units = len(order)
    nx = 4
    row, col = lax.axis_index("row"), lax.axis_index("col")
    x, hi = lax.rem(row, nx), lax.div(row, nx)
    nz = units // 2
    z, y_own = lax.rem(col, nz), lax.div(col, nz)
    starts = []
    for d, u in order:
        half = y_own if u == 0 else 1 - y_own
        starts.append(half * (nz * unit_rows) + lax.rem(z + d + nz, nz) * unit_rows)
    starts = [pl.multiple_of(p, unit_rows) for p in starts]
    copies = []

    def bring(src, dst):
        copies.append(pltpu.make_async_copy(src, dst, in_sem.at[len(copies)]))

    for j, piece in enumerate(pieces):
        shift, first_u = ((0, 0), (nx - 1, 0), (1, 0), (2, 0), (2, 1))[j % 5]
        sender = lax.rem(x + shift, nx)
        rows = piece.shape[0]
        for u in range(rows // unit_rows):
            first = j // 5 * (units // 2) + first_u + u
            at = starts[first]
            for q in range(1, nx):
                at = jnp.where(sender == q, starts[first + 2 * q], at)
            at = pl.multiple_of(at, unit_rows)
            src = piece.at[pl.ds(u * unit_rows, unit_rows), pl.ds(0, width)]
            bring(src, qkv.at[pl.ds(at, unit_rows)])
        if j < 5:
            for u in range(2):
                at = ((hi if u == 0 else 1 - hi) * nx + sender) * out_rows + first_u * unit_rows
                src = piece.at[:, pl.ds(width + u * heads * HD, heads * HD)]
                bring(src, og.at[pl.ds(pl.multiple_of(at, unit_rows), rows)])
    for c in copies:
        c.start()
    for c in copies:
        c.wait()
    w_copy = pltpu.make_async_copy(w_hbm, w, w_sem)
    w_copy.start()
    inv_root = 1.0 / math.sqrt(HD)
    to_base2 = inv_root * math.log2(math.e)
    nt = (((1,), (1,)), ((), ()))
    nn = (((1,), (0,)), ((), ()))
    half = QB // 2
    key_pos = lax.broadcasted_iota(jnp.int32, (half, half), 0)
    visible = key_pos <= lax.broadcasted_iota(jnp.int32, (half, half), 1)
    hidden = F32(-1e30)

    def dot(a, b, dims):
        return lax.dot_general(a, b, dims, preferred_element_type=F32)

    def join(*parts, axis=1):
        return jnp.concatenate(parts, axis=axis)

    for i in reversed(range(seq // QB)):
        rows, end = slice(i * QB, (i + 1) * QB), (i + 1) * QB
        lo = end - half
        for h in range(heads):
            base = h * 3 * HD
            k_t = qkv[:end, base + HD : base + 2 * HD].T
            v_t = qkv[:end, base + 2 * HD : base + 3 * HD].T
            q = qkv[rows, base : base + HD]
            k = qkv[:end, base + HD : base + 2 * HD]
            v = qkv[:end, base + 2 * HD : base + 3 * HD]
            g = og[rows, h * HD : (h + 1) * HD]
            s1 = dot(k[:lo], q, nt)
            s2 = jnp.where(visible, dot(k[lo:], q[half:], nt), hidden)
            edge = join(jnp.where(visible, s1[lo - half :, :half], hidden), s1[lo - half :, half:])
            s1 = edge if lo == half else join(s1[: lo - half], edge, axis=0)
            top1 = jnp.max(s1, axis=0, keepdims=True)
            top2 = jnp.max(s2, axis=0, keepdims=True)
            top = join(top1[:, :half], jnp.maximum(top1[:, half:], top2))
            e1 = jnp.exp2((s1 - top) * to_base2)
            e2 = jnp.exp2((s2 - top[:, half:]) * to_base2)
            sum1 = jnp.sum(e1, axis=0, keepdims=True)
            sum2 = jnp.sum(e2, axis=0, keepdims=True)
            inv = 1.0 / join(sum1[:, :half], sum1[:, half:] + sum2)
            p1, p2 = e1 * inv, e2 * inv[:, half:]
            b1, b2 = p1.astype(BF16), p2.astype(BF16)
            at = dot(v_t[:, :lo], b1, nn)
            at = join(at[:, :half], at[:, half:] + dot(v_t[:, lo:], b2, nn)).astype(BF16)
            dots = jnp.sum(g.T.astype(F32) * at.astype(F32), axis=0, keepdims=True)
            att[rows, h * HD : (h + 1) * HD] = at.T
            d1 = (p1 * (dot(v[:lo], g, nt) - dots)).astype(BF16)
            d2 = (p2 * (dot(v[lo:], g[half:], nt) - dots[:, half:])).astype(BF16)
            dq = dot(k_t[:, :lo], d1, nn)
            dq = join(dq[:, :half], dq[:, half:] + dot(k_t[:, lo:], d2, nn)) * inv_root
            grad[rows, base : base + HD] = dq.astype(BF16).T
            for acc, x1, x2, y in ((dk_acc, d1, d2, q), (dv_acc, b1, b2, g)):
                first, last = dot(x1, y, nn), dot(x2, y[half:], nn)
                if end == seq:
                    acc[h, :lo] = first
                    acc[h, lo:end] = last
                else:
                    acc[h, :lo] += first
                    acc[h, lo:end] += last
    for h in range(heads):
        base = h * 3 * HD
        grad[:, base + HD : base + 2 * HD] = (dk_acc[h] * inv_root).astype(BF16)
        grad[:, base + 2 * HD : base + 3 * HD] = dv_acc[h].astype(BF16)

    outs = [
        pltpu.make_async_copy(
            att.at[pl.ds(pl.multiple_of(row * out_rows, out_rows), out_rows)],
            att_out,
            out_sem.at[units],
        )
    ]
    for j in range(units):
        outs.append(
            pltpu.make_async_copy(
                grad.at[pl.ds(starts[j], unit_rows)],
                grad_out.at[pl.ds(j * unit_rows, unit_rows)],
                out_sem.at[j],
            )
        )
    for c in outs:
        c.start()
    w_copy.wait()
    tile = w.shape[0] // 2
    for first in reversed(range(0, units, 4)):
        group = range(first, first + 4)
        rows = jnp.concatenate([grad[pl.ds(starts[j], unit_rows)] for j in group], axis=0)
        for n in range(2):
            cols = slice(n * tile, (n + 1) * tile)
            y = dot(rows, w[cols], nt).astype(BF16)
            for i, j in enumerate(group):
                g_outs[j][:, cols] = y[i * unit_rows : (i + 1) * unit_rows]
    for c in outs:
        c.wait()


def attention(order, unit_rows, pieces, w_qkv, own_rows):
    depth, width = w_qkv.shape
    seq = sum(p.shape[0] for p in pieces)
    units = seq // unit_rows
    heads = width // (3 * HD)
    hbm = pl.BlockSpec(memory_space=pltpu.HBM)
    vmem = pl.BlockSpec(memory_space=pltpu.VMEM)
    attended, grads, *parts = pl.pallas_call(
        functools.partial(attention_kernel, heads, order, unit_rows),
        out_shape=[
            pltpu.HBM((own_rows, heads * HD), BF16),
            pltpu.HBM((seq, width), BF16),
        ]
        + [jax.ShapeDtypeStruct((unit_rows, depth), BF16)] * units,
        in_specs=[hbm] * (len(pieces) + 1),
        out_specs=[hbm, hbm] + [vmem] * units,
        scratch_shapes=[
            pltpu.VMEM((seq, width), BF16),
            pltpu.VMEM((seq, heads * HD), BF16),
            pltpu.VMEM((seq, heads * HD), BF16),
            pltpu.VMEM((seq, width), BF16),
            pltpu.VMEM((heads, seq, HD), F32),
            pltpu.VMEM((heads, seq, HD), F32),
            pltpu.VMEM((depth, width), BF16),
            pltpu.SemaphoreType.DMA((units + len(pieces),)),
            pltpu.SemaphoreType.DMA,
            pltpu.SemaphoreType.DMA((units + 1,)),
        ],
        compiler_params=pltpu.CompilerParams(vmem_limit_bytes=50 * 1024 * 1024),
        cost_estimate=pl.CostEstimate(
            flops=12 * heads * seq * seq * HD * 5 // 8,
            bytes_accessed=2 * seq * (width * 2 + heads * HD * 2),
            transcendentals=heads * seq * seq * 5 // 8,
        ),
    )(*pieces, w_qkv)
    return attended, grads, list(parts)


def per_device(inputs, w_qkv, out_grad):
    tok = inputs.shape[0]
    own_rows = out_grad.shape[0]
    rows = lax.axis_size("row")
    cols = lax.axis_size("col")
    nz = cols // 2
    seq = cols * tok

    def along_z(step):
        return [(y * nz + a, y * nz + (a + step) % nz) for y in range(2) for a in range(nz)]

    def up(v):
        return lax.ppermute(v, "col", along_z(1))

    def down(v):
        return lax.ppermute(v, "col", along_z(-1))

    def swap_y(v):
        return lax.ppermute(v, "col", [(c, (c + nz) % cols) for c in range(cols)])

    nx = rows // 2

    def along_x(v, step):
        perm = [(y * nx + a, y * nx + (a + step) % nx) for y in range(2) for a in range(nx)]
        return lax.ppermute(v, "row", perm)

    def swap_hi(v):
        return lax.ppermute(v, "row", [(r, (r + nx) % rows) for r in range(rows)])

    def add(*parts):
        return sum(p.astype(F32) for p in parts).astype(BF16)

    def over_x(parts):
        own, above, below, opposite_up, opposite_down = parts
        from_below, from_above = along_x(opposite_up, 1), along_x(opposite_down, nx - 1)
        above, below = add_half(above, from_below, 0), add_half(below, from_above, 1)
        return [own, along_x(above, 1), along_x(below, nx - 1)]

    def to_x(own):
        below, above = along_x(own, 1), along_x(own, nx - 1)
        half = own.shape[0] // 2
        opposite = [along_x(below[:half], 1), along_x(above[half:], nx - 1)]
        return [own, below, above] + opposite

    a0 = inputs
    w_vmem = hold(w_qkv)
    c0 = swap_y(inputs)
    af1, ab1 = up(a0), down(a0)
    c0, w_vmem = lax.optimization_barrier((c0, w_vmem))
    cf1, cb1 = up(c0), down(c0)
    af2, ab2 = up(af1), down(ab1)
    units = [a0, c0, af1, ab1, cf1, cb1, af2, ab2]
    parts, x_all = project(units, w_vmem, seq, 0)
    cf2, cb2 = up(cf1), down(cb1)
    af3, ab3 = up(af2), down(ab2)
    cf2, cb2, *parts = lax.optimization_barrier((cf2, cb2, *parts))
    cf3, cb3 = up(cf2), down(cb2)
    a4, c4 = up(af3), down(cb3)
    order = [(0, 0), (0, 1), (-1, 0), (1, 0), (-1, 1), (1, 1), (-2, 0), (2, 0)]
    order += [(-2, 1), (2, 1), (3, 0), (-3, 1), (-3, 0), (3, 1), (4, 0), (4, 1)]
    width = w_qkv.shape[1]
    got = over_x(parts)
    got[0], cf3, cb3 = lax.optimization_barrier((got[0], cf3, cb3))
    mine = sum_beside(got, out_grad)
    other = swap_hi(mine)
    other, a4, c4 = lax.optimization_barrier((other, a4, c4))
    summed = merge(mine, other, width)
    pieces = to_x(summed)
    units = [cf2, cb2, ab3, cf3, af3, cb3, a4, c4]
    parts, x_all = project(units, w_vmem, seq, seq // 2, x_all)
    *parts, summed = lax.optimization_barrier((*parts, summed))
    mine = add(*over_x(parts))
    pieces += to_x(add(mine, swap_hi(mine)))

    attended, grads, g = attention(order, tok, pieces, w_qkv, own_rows)
    g = dict(zip(order, g))

    c_down, a_up = down(g[4, 1]), up(g[4, 0])
    c_up, a_down = up(g[3, 1]), down(g[-3, 0])
    c_down, a_up = down(add(g[-3, 1], c_down)), up(add(g[3, 0], a_up))
    c_up, a_down = up(add(g[2, 1], c_up)), down(add(g[-2, 0], a_down))
    c_down, a_up = down(add(g[-2, 1], c_down)), up(add(g[2, 0], a_up))
    c_up, a_down = up(add(g[1, 1], c_up)), down(add(g[-1, 0], a_down))
    c_down, a_up = down(add(g[-1, 1], c_down)), up(add(g[1, 0], a_up))
    other = swap_y(add(g[0, 1], c_up, c_down))
    input_grad = add(g[0, 0], a_up, a_down, other)

    weight_grad = lax.dot_general(
        x_all, grads, (((0,), (0,)), ((), ())), preferred_element_type=F32
    ).astype(BF16)
    return attended, input_grad, weight_grad


def solution(mesh):
    placed = (P(("rep", "col"), "row"), P("row", "col"), P(("rep", "row"), "col"))
    return jax.shard_map(
        per_device,
        mesh=mesh,
        in_specs=placed,
        out_specs=(P(("rep", "row"), "col"), P(("rep", "col"), "row"), P(("rep", "row"), "col")),
        check_vma=False,
    )
```

```python
import functools
import math

import jax
import jax.numpy as jnp
from jax import lax
from jax.experimental import pallas as pl
from jax.experimental.pallas import tpu as pltpu
from jax.sharding import PartitionSpec as P

HD = 128
QB = 512
F32 = jnp.float32
BF16 = jnp.bfloat16


def hold_kernel(w_hbm, w, sem):
    step = w.shape[0] // sem.shape[0]
    copies = [
        pltpu.make_async_copy(w_hbm.at[pl.ds(i * step, step)], w.at[pl.ds(i * step, step)], sem.at[i])
        for i in range(sem.shape[0])
    ]
    for c in copies:
        c.start()
    for c in copies:
        c.wait()


def hold(w_qkv):
    return pl.pallas_call(
        hold_kernel,
        out_shape=pltpu.VMEM(w_qkv.shape, BF16),
        in_specs=[pl.BlockSpec(memory_space=pltpu.HBM)],
        out_specs=pl.BlockSpec(memory_space=pltpu.VMEM),
        scratch_shapes=[pltpu.SemaphoreType.DMA((8,))],
    )(w_qkv)


def project_kernel(units, unit_rows, first_row, others, *refs):
    xs, w = refs[:units], refs[units]
    outs, x_all = refs[units + 1 + others : -6], refs[-6]
    x, y, in_sem, lay_sem, out_sem = refs[-5:]
    nx = units // 2
    me = lax.rem(lax.axis_index("row"), nx)
    slots = [2 * lax.rem(j // 2 + nx - me, nx) + j % 2 for j in range(units)]
    slots = [pl.multiple_of(slot * unit_rows, unit_rows) for slot in slots]

    def in_copy(j):
        return pltpu.make_async_copy(xs[j], x.at[pl.ds(slots[j], unit_rows)], in_sem.at[j])

    lays = [
        pltpu.make_async_copy(
            x.at[pl.ds(slots[j], unit_rows)],
            x_all.at[pl.ds(first_row + j * unit_rows, unit_rows)],
            lay_sem.at[j],
        )
        for j in range(units)
    ]
    for j in range(units):
        in_copy(j).start()
    for j in range(units):
        in_copy(j).wait()
    for c in lays:
        c.start()
    tile = 3 * HD
    rows = outs[0].shape[0]
    places = [0, rows, 3 * rows, 2 * rows, 2 * rows + rows // 2]
    sends = []
    for n in range(w.shape[1] // tile):
        cols = slice(n * tile, (n + 1) * tile)
        y[:, cols] = jnp.dot(x[...], w[:, cols], preferred_element_type=F32).astype(BF16)
        for i, out in enumerate(outs):
            src = y.at[pl.ds(places[i], out.shape[0]), pl.ds(n * tile, tile)]
            sends.append(
                pltpu.make_async_copy(src, out.at[:, pl.ds(n * tile, tile)], out_sem.at[n, i])
            )
            sends[-1].start()
    for c in lays + sends:
        c.wait()


def project(xs, w_vmem, seq, first_row, x_all=None, after=()):
    units, (unit_rows, depth), width = len(xs), xs[0].shape, w_vmem.shape[1]
    hbm = pl.BlockSpec(memory_space=pltpu.HBM)
    others = ([] if x_all is None else [x_all]) + list(after)
    quarter = pltpu.HBM((units * unit_rows // 4, width), BF16)
    half = pltpu.HBM((units * unit_rows // 8, width), BF16)
    xs = [pltpu.with_memory_space_constraint(v, pltpu.HBM) for v in xs]
    *parts, x_all = pl.pallas_call(
        functools.partial(project_kernel, units, unit_rows, first_row, len(others)),
        out_shape=[quarter] * 3 + [half] * 2 + [pltpu.HBM((seq, depth), BF16)],
        in_specs=[hbm] * units + [pl.BlockSpec(memory_space=pltpu.VMEM)] + [hbm] * len(others),
        out_specs=[hbm] * 6,
        scratch_shapes=[
            pltpu.VMEM((units * unit_rows, depth), BF16),
            pltpu.VMEM((units * unit_rows, width), BF16),
            pltpu.SemaphoreType.DMA((units,)),
            pltpu.SemaphoreType.DMA((units,)),
            pltpu.SemaphoreType.DMA((width // (3 * HD), 5)),
        ],
        input_output_aliases={} if x_all is None else {units + 1: 5},
        compiler_params=pltpu.CompilerParams(vmem_limit_bytes=24 * 1024 * 1024),
        cost_estimate=pl.CostEstimate(
            flops=2 * units * unit_rows * depth * width,
            bytes_accessed=2 * units * unit_rows * (2 * depth + width),
            transcendentals=0,
        ),
    )(*xs, w_vmem, *others)
    return parts, x_all


def add_halves_kernel(above, below, from_below, from_above, above_out, below_out):
    first = pl.program_id(0) == 0

    @pl.when(first)
    def _():
        above_out[...] = (above[...].astype(F32) + from_below[...].astype(F32)).astype(BF16)
        below_out[...] = below[...]

    @pl.when(jnp.logical_not(first))
    def _():
        above_out[...] = above[...]
        below_out[...] = (below[...].astype(F32) + from_above[...].astype(F32)).astype(BF16)


def add_halves(above, below, from_below, from_above):
    half = pl.BlockSpec(from_below.shape, lambda i: (0, 0))
    return pl.pallas_call(
        add_halves_kernel,
        grid=(2,),
        out_shape=[jax.ShapeDtypeStruct(above.shape, BF16)] * 2,
        in_specs=[by_rows(above), by_rows(below), half, half],
        out_specs=[by_rows(above)] * 2,
    )(above, below, from_below, from_above)


def sum_beside_kernel(count, *refs):
    total = refs[0][...].astype(F32)
    for r in refs[1:count]:
        total = total + r[...].astype(F32)
    width = total.shape[1]
    out = refs[-1]
    out[:, :width] = total.astype(BF16)
    out[:, width:] = refs[count][...]


def by_rows(array, steps=2):
    rows, width = array.shape
    return pl.BlockSpec((rows // steps, width), lambda i: (i, 0))


def sum_beside(parts, beside):
    rows, width = parts[0].shape
    out = jax.ShapeDtypeStruct((rows, width + beside.shape[1]), BF16)
    return pl.pallas_call(
        functools.partial(sum_beside_kernel, len(parts)),
        grid=(2,),
        out_shape=out,
        in_specs=[by_rows(p) for p in (*parts, beside)],
        out_specs=by_rows(out),
    )(*parts, beside)


def merge_kernel(width, mine, got, out):
    total = mine[:, :width].astype(F32) + got[:, :width].astype(F32)
    out[:, :width] = total.astype(BF16)
    out[:, width : mine.shape[1]] = mine[:, width:]
    out[:, mine.shape[1] :] = got[:, width:]


def merge(mine, got, width):
    rows, both = mine.shape
    out = jax.ShapeDtypeStruct((rows, 2 * both - width), BF16)
    return pl.pallas_call(
        functools.partial(merge_kernel, width),
        grid=(2,),
        out_shape=out,
        in_specs=[by_rows(mine), by_rows(got)],
        out_specs=by_rows(out),
    )(mine, got)


def attention_kernel(heads, order, unit_rows, *refs):
    pieces, (w_hbm, att_out, grad_out) = refs[:10], refs[10:13]
    g_outs = refs[13 : 13 + len(order)]
    qkv, og, att, grad, dk_acc, dv_acc, w, in_sem, w_sem, out_sem = refs[13 + len(order) :]
    seq, width = qkv.shape
    out_rows = att_out.shape[0]
    units = len(order)
    nx = 4
    row, col = lax.axis_index("row"), lax.axis_index("col")
    x, hi = lax.rem(row, nx), lax.div(row, nx)
    nz = units // 2
    z, y_own = lax.rem(col, nz), lax.div(col, nz)
    starts = []
    for d, u in order:
        half = y_own if u == 0 else 1 - y_own
        starts.append(half * (nz * unit_rows) + lax.rem(z + d + nz, nz) * unit_rows)
    starts = [pl.multiple_of(p, unit_rows) for p in starts]
    copies = []

    def bring(src, dst):
        copies.append(pltpu.make_async_copy(src, dst, in_sem.at[len(copies)]))

    for j, piece in enumerate(pieces):
        shift, first_u = ((0, 0), (nx - 1, 0), (1, 0), (2, 0), (2, 1))[j % 5]
        sender = lax.rem(x + shift, nx)
        rows = piece.shape[0]
        for u in range(rows // unit_rows):
            first = j // 5 * (units // 2) + first_u + u
            at = starts[first]
            for q in range(1, nx):
                at = jnp.where(sender == q, starts[first + 2 * q], at)
            at = pl.multiple_of(at, unit_rows)
            src = piece.at[pl.ds(u * unit_rows, unit_rows), pl.ds(0, width)]
            bring(src, qkv.at[pl.ds(at, unit_rows)])
        if j < 5:
            for u in range(2):
                at = ((hi if u == 0 else 1 - hi) * nx + sender) * out_rows + first_u * unit_rows
                src = piece.at[:, pl.ds(width + u * heads * HD, heads * HD)]
                bring(src, og.at[pl.ds(pl.multiple_of(at, unit_rows), rows)])
    for c in copies:
        c.start()
    for c in copies:
        c.wait()
    w_copy = pltpu.make_async_copy(w_hbm, w, w_sem)
    w_copy.start()
    inv_root = 1.0 / math.sqrt(HD)
    to_base2 = inv_root * math.log2(math.e)
    nt = (((1,), (1,)), ((), ()))
    nn = (((1,), (0,)), ((), ()))
    half = QB // 2
    key_pos = lax.broadcasted_iota(jnp.int32, (half, half), 0)
    visible = key_pos <= lax.broadcasted_iota(jnp.int32, (half, half), 1)
    hidden = F32(-1e30)

    def dot(a, b, dims):
        return lax.dot_general(a, b, dims, preferred_element_type=F32)

    def join(*parts, axis=1):
        return jnp.concatenate(parts, axis=axis)

    for i in reversed(range(seq // QB)):
        rows, end = slice(i * QB, (i + 1) * QB), (i + 1) * QB
        lo = end - half
        for h in range(heads):
            base = h * 3 * HD
            k_t = qkv[:end, base + HD : base + 2 * HD].T
            v_t = qkv[:end, base + 2 * HD : base + 3 * HD].T
            q = qkv[rows, base : base + HD]
            k = qkv[:end, base + HD : base + 2 * HD]
            v = qkv[:end, base + 2 * HD : base + 3 * HD]
            g = og[rows, h * HD : (h + 1) * HD]
            s1 = dot(k[:lo], q, nt)
            s2 = jnp.where(visible, dot(k[lo:], q[half:], nt), hidden)
            edge = join(jnp.where(visible, s1[lo - half :, :half], hidden), s1[lo - half :, half:])
            s1 = edge if lo == half else join(s1[: lo - half], edge, axis=0)
            top1 = jnp.max(s1, axis=0, keepdims=True)
            top2 = jnp.max(s2, axis=0, keepdims=True)
            top = join(top1[:, :half], jnp.maximum(top1[:, half:], top2))
            e1 = jnp.exp2((s1 - top) * to_base2)
            e2 = jnp.exp2((s2 - top[:, half:]) * to_base2)
            sum1 = jnp.sum(e1, axis=0, keepdims=True)
            sum2 = jnp.sum(e2, axis=0, keepdims=True)
            inv = 1.0 / join(sum1[:, :half], sum1[:, half:] + sum2)
            p1, p2 = e1 * inv, e2 * inv[:, half:]
            b1, b2 = p1.astype(BF16), p2.astype(BF16)
            at = dot(v_t[:, :lo], b1, nn)
            at = join(at[:, :half], at[:, half:] + dot(v_t[:, lo:], b2, nn)).astype(BF16)
            dots = jnp.sum(g.T.astype(F32) * at.astype(F32), axis=0, keepdims=True)
            att[rows, h * HD : (h + 1) * HD] = at.T
            d1 = (p1 * (dot(v[:lo], g, nt) - dots)).astype(BF16)
            d2 = (p2 * (dot(v[lo:], g[half:], nt) - dots[:, half:])).astype(BF16)
            dq = dot(k_t[:, :lo], d1, nn)
            dq = join(dq[:, :half], dq[:, half:] + dot(k_t[:, lo:], d2, nn)) * inv_root
            grad[rows, base : base + HD] = dq.astype(BF16).T
            for acc, x1, x2, y in ((dk_acc, d1, d2, q), (dv_acc, b1, b2, g)):
                first, last = dot(x1, y, nn), dot(x2, y[half:], nn)
                if end == seq:
                    acc[h, :lo] = first
                    acc[h, lo:end] = last
                else:
                    acc[h, :lo] += first
                    acc[h, lo:end] += last
    for h in range(heads):
        base = h * 3 * HD
        grad[:, base + HD : base + 2 * HD] = (dk_acc[h] * inv_root).astype(BF16)
        grad[:, base + 2 * HD : base + 3 * HD] = dv_acc[h].astype(BF16)

    outs = [
        pltpu.make_async_copy(
            att.at[pl.ds(pl.multiple_of(row * out_rows, out_rows), out_rows)],
            att_out,
            out_sem.at[units],
        )
    ]
    for j in range(units):
        outs.append(
            pltpu.make_async_copy(
                grad.at[pl.ds(starts[j], unit_rows)],
                grad_out.at[pl.ds(j * unit_rows, unit_rows)],
                out_sem.at[j],
            )
        )
    for c in outs:
        c.start()
    w_copy.wait()
    tile = w.shape[0] // 2
    for first in reversed(range(0, units, 4)):
        group = range(first, first + 4)
        rows = jnp.concatenate([grad[pl.ds(starts[j], unit_rows)] for j in group], axis=0)
        for n in range(2):
            cols = slice(n * tile, (n + 1) * tile)
            y = dot(rows, w[cols], nt).astype(BF16)
            for i, j in enumerate(group):
                g_outs[j][:, cols] = y[i * unit_rows : (i + 1) * unit_rows]
    for c in outs:
        c.wait()


def attention(order, unit_rows, pieces, w_qkv, own_rows):
    depth, width = w_qkv.shape
    seq = sum(p.shape[0] for p in pieces)
    units = seq // unit_rows
    heads = width // (3 * HD)
    hbm = pl.BlockSpec(memory_space=pltpu.HBM)
    vmem = pl.BlockSpec(memory_space=pltpu.VMEM)
    attended, grads, *parts = pl.pallas_call(
        functools.partial(attention_kernel, heads, order, unit_rows),
        out_shape=[
            pltpu.HBM((own_rows, heads * HD), BF16),
            pltpu.HBM((seq, width), BF16),
        ]
        + [jax.ShapeDtypeStruct((unit_rows, depth), BF16)] * units,
        in_specs=[hbm] * (len(pieces) + 1),
        out_specs=[hbm, hbm] + [vmem] * units,
        scratch_shapes=[
            pltpu.VMEM((seq, width), BF16),
            pltpu.VMEM((seq, heads * HD), BF16),
            pltpu.VMEM((seq, heads * HD), BF16),
            pltpu.VMEM((seq, width), BF16),
            pltpu.VMEM((heads, seq, HD), F32),
            pltpu.VMEM((heads, seq, HD), F32),
            pltpu.VMEM((depth, width), BF16),
            pltpu.SemaphoreType.DMA((units + len(pieces),)),
            pltpu.SemaphoreType.DMA,
            pltpu.SemaphoreType.DMA((units + 1,)),
        ],
        compiler_params=pltpu.CompilerParams(vmem_limit_bytes=50 * 1024 * 1024),
        cost_estimate=pl.CostEstimate(
            flops=12 * heads * seq * seq * HD * 5 // 8,
            bytes_accessed=2 * seq * (width * 2 + heads * HD * 2),
            transcendentals=heads * seq * seq * 5 // 8,
        ),
    )(*pieces, w_qkv)
    return attended, grads, list(parts)


def per_device(inputs, w_qkv, out_grad):
    tok = inputs.shape[0]
    own_rows = out_grad.shape[0]
    rows = lax.axis_size("row")
    cols = lax.axis_size("col")
    nz = cols // 2
    seq = cols * tok

    def along_z(step):
        return [(y * nz + a, y * nz + (a + step) % nz) for y in range(2) for a in range(nz)]

    def up(v):
        return lax.ppermute(v, "col", along_z(1))

    def down(v):
        return lax.ppermute(v, "col", along_z(-1))

    def swap_y(v):
        return lax.ppermute(v, "col", [(c, (c + nz) % cols) for c in range(cols)])

    nx = rows // 2

    def along_x(v, step):
        perm = [(y * nx + a, y * nx + (a + step) % nx) for y in range(2) for a in range(nx)]
        return lax.ppermute(v, "row", perm)

    def swap_hi(v):
        return lax.ppermute(v, "row", [(r, (r + nx) % rows) for r in range(rows)])

    def add(*parts):
        return sum(p.astype(F32) for p in parts).astype(BF16)

    def over_x(parts, *before):
        own, above, below, opposite_up, opposite_down = parts
        got = along_x(opposite_up, 1), along_x(opposite_down, nx - 1)
        *got, before = lax.optimization_barrier((*got, before))
        above, below = add_halves(above, below, *got)
        return [own, along_x(above, 1), along_x(below, nx - 1)], before

    def to_x(own):
        below, above = along_x(own, 1), along_x(own, nx - 1)
        half = own.shape[0] // 2
        opposite = [along_x(below[:half], 1), along_x(above[half:], nx - 1)]
        return [own, below, above] + opposite

    a0 = inputs
    w_vmem = hold(w_qkv)
    c0 = swap_y(inputs)
    af1, ab1 = up(a0), down(a0)
    c0, w_vmem = lax.optimization_barrier((c0, w_vmem))
    cf1, cb1 = up(c0), down(c0)
    af2, ab2 = up(af1), down(ab1)
    units = [a0, c0, af1, ab1, cf1, cb1, af2, ab2]
    parts, x_all = project(units, w_vmem, seq, 0)
    cf2, cb2 = up(cf1), down(cb1)
    af3, ab3 = up(af2), down(ab2)
    cf2, cb2, *parts = lax.optimization_barrier((cf2, cb2, *parts))
    cf3, cb3 = up(cf2), down(cb2)
    order = [(0, 0), (0, 1), (-1, 0), (1, 0), (-1, 1), (1, 1), (-2, 0), (2, 0)]
    order += [(-2, 1), (2, 1), (3, 0), (-3, 1), (-3, 0), (3, 1), (4, 0), (4, 1)]
    width = w_qkv.shape[1]
    got, (cf3, cb3) = over_x(parts, cf3, cb3)
    a4, c4 = up(af3), down(cb3)
    got[0], a4, c4 = lax.optimization_barrier((got[0], a4, c4))
    mine = sum_beside(got, out_grad)
    units = [cf2, cb2, ab3, cf3, af3, cb3, a4, c4]
    parts, x_all = project(units, w_vmem, seq, seq // 2, x_all)
    *parts, mine = lax.optimization_barrier((*parts, mine))
    got, (other,) = over_x(parts, swap_hi(mine))
    pieces = to_x(merge(mine, other, width))
    got[0], pieces[1], pieces[2] = lax.optimization_barrier((got[0], pieces[1], pieces[2]))
    mine = add(*got)
    pieces += to_x(add(mine, swap_hi(mine)))

    attended, grads, g = attention(order, tok, pieces, w_qkv, own_rows)
    g = dict(zip(order, g))

    c_down, a_up = down(g[4, 1]), up(g[4, 0])
    c_up, a_down = up(g[3, 1]), down(g[-3, 0])
    c_down, a_up = down(add(g[-3, 1], c_down)), up(add(g[3, 0], a_up))
    c_up, a_down = up(add(g[2, 1], c_up)), down(add(g[-2, 0], a_down))
    c_down, a_up = down(add(g[-2, 1], c_down)), up(add(g[2, 0], a_up))
    c_up, a_down = up(add(g[1, 1], c_up)), down(add(g[-1, 0], a_down))
    c_down, a_up = down(add(g[-1, 1], c_down)), up(add(g[1, 0], a_up))
    other = swap_y(add(g[0, 1], c_up, c_down))
    input_grad = add(g[0, 0], a_up, a_down, other)

    weight_grad = lax.dot_general(
        x_all, grads, (((0,), (0,)), ((), ())), preferred_element_type=F32
    ).astype(BF16)
    return attended, input_grad, weight_grad


def solution(mesh):
    placed = (P(("rep", "col"), "row"), P("row", "col"), P(("rep", "row"), "col"))
    return jax.shard_map(
        per_device,
        mesh=mesh,
        in_specs=placed,
        out_specs=(P(("rep", "row"), "col"), P(("rep", "col"), "row"), P(("rep", "row"), "col")),
        check_vma=False,
    )
```

```python
import functools
import math

import jax
import jax.numpy as jnp
from jax import lax
from jax.experimental import pallas as pl
from jax.experimental.pallas import tpu as pltpu
from jax.sharding import PartitionSpec as P

HD = 128
QB = 512
F32 = jnp.float32
BF16 = jnp.bfloat16


def hold_kernel(w_hbm, w, sem):
    step = w.shape[0] // sem.shape[0]
    copies = [
        pltpu.make_async_copy(w_hbm.at[pl.ds(i * step, step)], w.at[pl.ds(i * step, step)], sem.at[i])
        for i in range(sem.shape[0])
    ]
    for c in copies:
        c.start()
    for c in copies:
        c.wait()


def hold(w_qkv):
    return pl.pallas_call(
        hold_kernel,
        out_shape=pltpu.VMEM(w_qkv.shape, BF16),
        in_specs=[pl.BlockSpec(memory_space=pltpu.HBM)],
        out_specs=pl.BlockSpec(memory_space=pltpu.VMEM),
        scratch_shapes=[pltpu.SemaphoreType.DMA((8,))],
    )(w_qkv)


def project_kernel(units, unit_rows, first_row, others, *refs):
    xs, w = refs[:units], refs[units]
    outs, x_all = refs[units + 1 + others : -6], refs[-6]
    x, y, in_sem, lay_sem, out_sem = refs[-5:]
    nx = units // 2
    me = lax.rem(lax.axis_index("row"), nx)
    slots = [2 * lax.rem(j // 2 + nx - me, nx) + j % 2 for j in range(units)]

    def in_copy(j, slot):
        return pltpu.make_async_copy(
            xs[j], x.at[pl.ds(slot * unit_rows, unit_rows)], in_sem.at[slot]
        )

    lays = [
        pltpu.make_async_copy(
            x.at[pl.ds(slots[j] * unit_rows, unit_rows)],
            x_all.at[pl.ds(first_row + j * unit_rows, unit_rows)],
            lay_sem.at[j],
        )
        for j in range(units)
    ]
    for j in range(units):
        in_copy(j, slots[j]).start()
    rows = outs[0].shape[0]
    places = [0, rows, 3 * rows, 2 * rows, 2 * rows + rows // 2]
    group = 2 * rows
    sends = []
    for start in range(0, 4 * rows, group):
        for slot in range(start // unit_rows, (start + group) // unit_rows):
            in_copy(0, slot).wait()
        here = slice(start, start + group)
        y[here] = jnp.dot(x[here], w[...], preferred_element_type=F32).astype(BF16)
        for i, out in enumerate(outs):
            if start <= places[i] < start + group:
                src = y.at[pl.ds(places[i], out.shape[0])]
                sends.append(pltpu.make_async_copy(src, out, out_sem.at[i]))
                sends[-1].start()
    for c in lays:
        c.start()
    for c in lays + sends:
        c.wait()


def project(xs, w_vmem, seq, first_row, x_all=None, after=()):
    units, (unit_rows, depth), width = len(xs), xs[0].shape, w_vmem.shape[1]
    hbm = pl.BlockSpec(memory_space=pltpu.HBM)
    others = ([] if x_all is None else [x_all]) + list(after)
    quarter = pltpu.HBM((units * unit_rows // 4, width), BF16)
    half = pltpu.HBM((units * unit_rows // 8, width), BF16)
    xs = [pltpu.with_memory_space_constraint(v, pltpu.HBM) for v in xs]
    *parts, x_all = pl.pallas_call(
        functools.partial(project_kernel, units, unit_rows, first_row, len(others)),
        out_shape=[quarter] * 3 + [half] * 2 + [pltpu.HBM((seq, depth), BF16)],
        in_specs=[hbm] * units + [pl.BlockSpec(memory_space=pltpu.VMEM)] + [hbm] * len(others),
        out_specs=[hbm] * 6,
        scratch_shapes=[
            pltpu.VMEM((units * unit_rows, depth), BF16),
            pltpu.VMEM((units * unit_rows, width), BF16),
            pltpu.SemaphoreType.DMA((units,)),
            pltpu.SemaphoreType.DMA((units,)),
            pltpu.SemaphoreType.DMA((5,)),
        ],
        input_output_aliases={} if x_all is None else {units + 1: 5},
        compiler_params=pltpu.CompilerParams(vmem_limit_bytes=24 * 1024 * 1024),
        cost_estimate=pl.CostEstimate(
            flops=2 * units * unit_rows * depth * width,
            bytes_accessed=2 * units * unit_rows * (2 * depth + width),
            transcendentals=0,
        ),
    )(*xs, w_vmem, *others)
    return parts, x_all


def add_halves_kernel(above, below, from_below, from_above, above_out, below_out):
    first = pl.program_id(0) == 0

    @pl.when(first)
    def _():
        above_out[...] = (above[...].astype(F32) + from_below[...].astype(F32)).astype(BF16)
        below_out[...] = below[...]

    @pl.when(jnp.logical_not(first))
    def _():
        above_out[...] = above[...]
        below_out[...] = (below[...].astype(F32) + from_above[...].astype(F32)).astype(BF16)


def add_halves(above, below, from_below, from_above):
    half = pl.BlockSpec(from_below.shape, lambda i: (0, 0))
    return pl.pallas_call(
        add_halves_kernel,
        grid=(2,),
        out_shape=[jax.ShapeDtypeStruct(above.shape, BF16)] * 2,
        in_specs=[by_rows(above), by_rows(below), half, half],
        out_specs=[by_rows(above)] * 2,
    )(above, below, from_below, from_above)


def sum_beside_kernel(count, *refs):
    total = refs[0][...].astype(F32)
    for r in refs[1:count]:
        total = total + r[...].astype(F32)
    width = total.shape[1]
    out = refs[-1]
    out[:, :width] = total.astype(BF16)
    out[:, width:] = refs[count][...]


def by_rows(array, steps=2):
    rows, width = array.shape
    return pl.BlockSpec((rows // steps, width), lambda i: (i, 0))


def sum_beside(parts, beside):
    rows, width = parts[0].shape
    out = jax.ShapeDtypeStruct((rows, width + beside.shape[1]), BF16)
    return pl.pallas_call(
        functools.partial(sum_beside_kernel, len(parts)),
        grid=(2,),
        out_shape=out,
        in_specs=[by_rows(p) for p in (*parts, beside)],
        out_specs=by_rows(out),
    )(*parts, beside)


def merge_kernel(width, mine, got, out):
    total = mine[:, :width].astype(F32) + got[:, :width].astype(F32)
    out[:, :width] = total.astype(BF16)
    out[:, width : mine.shape[1]] = mine[:, width:]
    out[:, mine.shape[1] :] = got[:, width:]


def merge(mine, got, width):
    rows, both = mine.shape
    out = jax.ShapeDtypeStruct((rows, 2 * both - width), BF16)
    return pl.pallas_call(
        functools.partial(merge_kernel, width),
        grid=(2,),
        out_shape=out,
        in_specs=[by_rows(mine), by_rows(got)],
        out_specs=by_rows(out),
    )(mine, got)


def attention_kernel(heads, order, unit_rows, *refs):
    pieces, (w_hbm, att_out, grad_out) = refs[:10], refs[10:13]
    g_outs = refs[13 : 13 + len(order)]
    qkv, og, att, grad, dk_acc, dv_acc, w, in_sem, w_sem, out_sem = refs[13 + len(order) :]
    seq, width = qkv.shape
    out_rows = att_out.shape[0]
    units = len(order)
    nx = 4
    row, col = lax.axis_index("row"), lax.axis_index("col")
    x, hi = lax.rem(row, nx), lax.div(row, nx)
    nz = units // 2
    z, y_own = lax.rem(col, nz), lax.div(col, nz)
    starts = []
    for d, u in order:
        half = y_own if u == 0 else 1 - y_own
        starts.append(half * (nz * unit_rows) + lax.rem(z + d + nz, nz) * unit_rows)
    starts = [pl.multiple_of(p, unit_rows) for p in starts]
    copies = []

    def bring(src, dst):
        copies.append(pltpu.make_async_copy(src, dst, in_sem.at[len(copies)]))

    for j, piece in enumerate(pieces):
        shift, first_u = ((0, 0), (nx - 1, 0), (1, 0), (2, 0), (2, 1))[j % 5]
        sender = lax.rem(x + shift, nx)
        rows = piece.shape[0]
        for u in range(rows // unit_rows):
            first = j // 5 * (units // 2) + first_u + u
            at = starts[first]
            for q in range(1, nx):
                at = jnp.where(sender == q, starts[first + 2 * q], at)
            at = pl.multiple_of(at, unit_rows)
            src = piece.at[pl.ds(u * unit_rows, unit_rows), pl.ds(0, width)]
            bring(src, qkv.at[pl.ds(at, unit_rows)])
        if j < 5:
            for u in range(2):
                at = ((hi if u == 0 else 1 - hi) * nx + sender) * out_rows + first_u * unit_rows
                src = piece.at[:, pl.ds(width + u * heads * HD, heads * HD)]
                bring(src, og.at[pl.ds(pl.multiple_of(at, unit_rows), rows)])
    for c in copies:
        c.start()
    for c in copies:
        c.wait()
    w_copy = pltpu.make_async_copy(w_hbm, w, w_sem)
    w_copy.start()
    inv_root = 1.0 / math.sqrt(HD)
    to_base2 = inv_root * math.log2(math.e)
    nt = (((1,), (1,)), ((), ()))
    nn = (((1,), (0,)), ((), ()))
    half = QB // 2
    key_pos = lax.broadcasted_iota(jnp.int32, (half, half), 0)
    visible = key_pos <= lax.broadcasted_iota(jnp.int32, (half, half), 1)
    hidden = F32(-1e30)

    def dot(a, b, dims):
        return lax.dot_general(a, b, dims, preferred_element_type=F32)

    def join(*parts, axis=1):
        return jnp.concatenate(parts, axis=axis)

    for i in reversed(range(seq // QB)):
        rows, end = slice(i * QB, (i + 1) * QB), (i + 1) * QB
        lo = end - half
        for h in range(heads):
            base = h * 3 * HD
            k_t = qkv[:end, base + HD : base + 2 * HD].T
            v_t = qkv[:end, base + 2 * HD : base + 3 * HD].T
            q = qkv[rows, base : base + HD]
            k = qkv[:end, base + HD : base + 2 * HD]
            v = qkv[:end, base + 2 * HD : base + 3 * HD]
            g = og[rows, h * HD : (h + 1) * HD]
            s1 = dot(k[:lo], q, nt)
            s2 = jnp.where(visible, dot(k[lo:], q[half:], nt), hidden)
            edge = join(jnp.where(visible, s1[lo - half :, :half], hidden), s1[lo - half :, half:])
            s1 = edge if lo == half else join(s1[: lo - half], edge, axis=0)
            top1 = jnp.max(s1, axis=0, keepdims=True)
            top2 = jnp.max(s2, axis=0, keepdims=True)
            top = join(top1[:, :half], jnp.maximum(top1[:, half:], top2))
            e1 = jnp.exp2((s1 - top) * to_base2)
            e2 = jnp.exp2((s2 - top[:, half:]) * to_base2)
            sum1 = jnp.sum(e1, axis=0, keepdims=True)
            sum2 = jnp.sum(e2, axis=0, keepdims=True)
            inv = 1.0 / join(sum1[:, :half], sum1[:, half:] + sum2)
            p1, p2 = e1 * inv, e2 * inv[:, half:]
            b1, b2 = p1.astype(BF16), p2.astype(BF16)
            at = dot(v_t[:, :lo], b1, nn)
            at = join(at[:, :half], at[:, half:] + dot(v_t[:, lo:], b2, nn)).astype(BF16)
            dots = jnp.sum(g.T.astype(F32) * at.astype(F32), axis=0, keepdims=True)
            att[rows, h * HD : (h + 1) * HD] = at.T
            d1 = (p1 * (dot(v[:lo], g, nt) - dots)).astype(BF16)
            d2 = (p2 * (dot(v[lo:], g[half:], nt) - dots[:, half:])).astype(BF16)
            dq = dot(k_t[:, :lo], d1, nn)
            dq = join(dq[:, :half], dq[:, half:] + dot(k_t[:, lo:], d2, nn)) * inv_root
            grad[rows, base : base + HD] = dq.astype(BF16).T
            for acc, x1, x2, y in ((dk_acc, d1, d2, q), (dv_acc, b1, b2, g)):
                first, last = dot(x1, y, nn), dot(x2, y[half:], nn)
                if end == seq:
                    acc[h, :lo] = first
                    acc[h, lo:end] = last
                else:
                    acc[h, :lo] += first
                    acc[h, lo:end] += last
    for h in range(heads):
        base = h * 3 * HD
        grad[:, base + HD : base + 2 * HD] = (dk_acc[h] * inv_root).astype(BF16)
        grad[:, base + 2 * HD : base + 3 * HD] = dv_acc[h].astype(BF16)

    outs = [
        pltpu.make_async_copy(
            att.at[pl.ds(pl.multiple_of(row * out_rows, out_rows), out_rows)],
            att_out,
            out_sem.at[units],
        )
    ]
    for j in range(units):
        outs.append(
            pltpu.make_async_copy(
                grad.at[pl.ds(starts[j], unit_rows)],
                grad_out.at[pl.ds(j * unit_rows, unit_rows)],
                out_sem.at[j],
            )
        )
    for c in outs:
        c.start()
    w_copy.wait()
    tile = w.shape[0] // 2
    for first in reversed(range(0, units, 4)):
        group = range(first, first + 4)
        rows = jnp.concatenate([grad[pl.ds(starts[j], unit_rows)] for j in group], axis=0)
        for n in range(2):
            cols = slice(n * tile, (n + 1) * tile)
            y = dot(rows, w[cols], nt).astype(BF16)
            for i, j in enumerate(group):
                g_outs[j][:, cols] = y[i * unit_rows : (i + 1) * unit_rows]
    for c in outs:
        c.wait()


def attention(order, unit_rows, pieces, w_qkv, own_rows):
    depth, width = w_qkv.shape
    seq = sum(p.shape[0] for p in pieces)
    units = seq // unit_rows
    heads = width // (3 * HD)
    hbm = pl.BlockSpec(memory_space=pltpu.HBM)
    vmem = pl.BlockSpec(memory_space=pltpu.VMEM)
    attended, grads, *parts = pl.pallas_call(
        functools.partial(attention_kernel, heads, order, unit_rows),
        out_shape=[
            pltpu.HBM((own_rows, heads * HD), BF16),
            pltpu.HBM((seq, width), BF16),
        ]
        + [jax.ShapeDtypeStruct((unit_rows, depth), BF16)] * units,
        in_specs=[hbm] * (len(pieces) + 1),
        out_specs=[hbm, hbm] + [vmem] * units,
        scratch_shapes=[
            pltpu.VMEM((seq, width), BF16),
            pltpu.VMEM((seq, heads * HD), BF16),
            pltpu.VMEM((seq, heads * HD), BF16),
            pltpu.VMEM((seq, width), BF16),
            pltpu.VMEM((heads, seq, HD), F32),
            pltpu.VMEM((heads, seq, HD), F32),
            pltpu.VMEM((depth, width), BF16),
            pltpu.SemaphoreType.DMA((units + len(pieces),)),
            pltpu.SemaphoreType.DMA,
            pltpu.SemaphoreType.DMA((units + 1,)),
        ],
        compiler_params=pltpu.CompilerParams(vmem_limit_bytes=50 * 1024 * 1024),
        cost_estimate=pl.CostEstimate(
            flops=12 * heads * seq * seq * HD * 5 // 8,
            bytes_accessed=2 * seq * (width * 2 + heads * HD * 2),
            transcendentals=heads * seq * seq * 5 // 8,
        ),
    )(*pieces, w_qkv)
    return attended, grads, list(parts)


def per_device(inputs, w_qkv, out_grad):
    tok = inputs.shape[0]
    own_rows = out_grad.shape[0]
    rows = lax.axis_size("row")
    cols = lax.axis_size("col")
    nz = cols // 2
    seq = cols * tok

    def along_z(step):
        return [(y * nz + a, y * nz + (a + step) % nz) for y in range(2) for a in range(nz)]

    def up(v):
        return lax.ppermute(v, "col", along_z(1))

    def down(v):
        return lax.ppermute(v, "col", along_z(-1))

    def swap_y(v):
        return lax.ppermute(v, "col", [(c, (c + nz) % cols) for c in range(cols)])

    nx = rows // 2

    def along_x(v, step):
        perm = [(y * nx + a, y * nx + (a + step) % nx) for y in range(2) for a in range(nx)]
        return lax.ppermute(v, "row", perm)

    def swap_hi(v):
        return lax.ppermute(v, "row", [(r, (r + nx) % rows) for r in range(rows)])

    def add(*parts):
        return sum(p.astype(F32) for p in parts).astype(BF16)

    def over_x(parts, *before, later=()):
        own, above, below, opposite_up, opposite_down = parts
        got = along_x(opposite_up, 1), along_x(opposite_down, nx - 1)
        *got, before = lax.optimization_barrier((*got, before))
        above, below = add_halves(above, below, *got)
        if later:
            *later, above, below = lax.optimization_barrier((*later, above, below))
        return [own, along_x(above, 1), along_x(below, nx - 1)], (*before, *later)

    def to_x(own):
        below, above = along_x(own, 1), along_x(own, nx - 1)
        half = own.shape[0] // 2
        opposite = [along_x(below[:half], 1), along_x(above[half:], nx - 1)]
        return [own, below, above] + opposite

    a0 = inputs
    w_vmem = hold(w_qkv)
    c0 = swap_y(inputs)
    af1, ab1 = up(a0), down(a0)
    c0, w_vmem = lax.optimization_barrier((c0, w_vmem))
    cf1, cb1 = up(c0), down(c0)
    af2, ab2 = up(af1), down(ab1)
    units = [a0, c0, af1, ab1, cf1, cb1, af2, ab2]
    parts, x_all = project(units, w_vmem, seq, 0)
    cf2, cb2 = up(cf1), down(cb1)
    af3, ab3 = up(af2), down(ab2)
    cf2, cb2, *parts = lax.optimization_barrier((cf2, cb2, *parts))
    cf3, cb3 = up(cf2), down(cb2)
    order = [(0, 0), (0, 1), (-1, 0), (1, 0), (-1, 1), (1, 1), (-2, 0), (2, 0)]
    order += [(-2, 1), (2, 1), (3, 0), (-3, 1), (-3, 0), (3, 1), (4, 0), (4, 1)]
    width = w_qkv.shape[1]
    got, (cf3, cb3) = over_x(parts, cf3, cb3)
    a4, c4 = up(af3), down(cb3)
    got[0], a4, c4 = lax.optimization_barrier((got[0], a4, c4))
    mine = sum_beside(got, out_grad)
    units = [cf2, cb2, ab3, cf3, af3, cb3, a4, c4]
    parts, x_all = project(units, w_vmem, seq, seq // 2, x_all)
    *parts, mine = lax.optimization_barrier((*parts, mine))
    other = swap_hi(mine)
    got, (other,) = over_x(parts, other)
    pieces = to_x(merge(mine, other, width))
    got[0], pieces[1], pieces[2] = lax.optimization_barrier((got[0], pieces[1], pieces[2]))
    mine = add(*got)
    pieces += to_x(add(mine, swap_hi(mine)))

    attended, grads, g = attention(order, tok, pieces, w_qkv, own_rows)
    g = dict(zip(order, g))

    c_down, a_up = down(g[4, 1]), up(g[4, 0])
    c_up, a_down = up(g[3, 1]), down(g[-3, 0])
    c_down, a_up = down(add(g[-3, 1], c_down)), up(add(g[3, 0], a_up))
    c_up, a_down = up(add(g[2, 1], c_up)), down(add(g[-2, 0], a_down))
    c_down, a_up = down(add(g[-2, 1], c_down)), up(add(g[2, 0], a_up))
    c_up, a_down = up(add(g[1, 1], c_up)), down(add(g[-1, 0], a_down))
    c_down, a_up = down(add(g[-1, 1], c_down)), up(add(g[1, 0], a_up))
    other = swap_y(add(g[0, 1], c_up, c_down))
    input_grad = add(g[0, 0], a_up, a_down, other)

    weight_grad = lax.dot_general(
        x_all, grads, (((0,), (0,)), ((), ())), preferred_element_type=F32
    ).astype(BF16)
    return attended, input_grad, weight_grad


def solution(mesh):
    placed = (P(("rep", "col"), "row"), P("row", "col"), P(("rep", "row"), "col"))
    return jax.shard_map(
        per_device,
        mesh=mesh,
        in_specs=placed,
        out_specs=(P(("rep", "row"), "col"), P(("rep", "col"), "row"), P(("rep", "row"), "col")),
        check_vma=False,
    )
```

```python
import functools
import math

import jax
import jax.numpy as jnp
from jax import lax
from jax.experimental import pallas as pl
from jax.experimental.pallas import tpu as pltpu
from jax.sharding import PartitionSpec as P

HD = 128
QB = 512
F32 = jnp.float32
BF16 = jnp.bfloat16


def hold_kernel(w_hbm, w, sem):
    step = w.shape[0] // sem.shape[0]
    copies = [
        pltpu.make_async_copy(w_hbm.at[pl.ds(i * step, step)], w.at[pl.ds(i * step, step)], sem.at[i])
        for i in range(sem.shape[0])
    ]
    for c in copies:
        c.start()
    for c in copies:
        c.wait()


def hold(w_qkv):
    return pl.pallas_call(
        hold_kernel,
        out_shape=pltpu.VMEM(w_qkv.shape, BF16),
        in_specs=[pl.BlockSpec(memory_space=pltpu.HBM)],
        out_specs=pl.BlockSpec(memory_space=pltpu.VMEM),
        scratch_shapes=[pltpu.SemaphoreType.DMA((8,))],
    )(w_qkv)


def project_kernel(units, unit_rows, first_row, others, *refs):
    xs, w = refs[:units], refs[units]
    outs, x_all = refs[units + 1 + others : -6], refs[-6]
    x, y, in_sem, lay_sem, out_sem = refs[-5:]
    nx = units // 2
    me = lax.rem(lax.axis_index("row"), nx)
    slots = [2 * lax.rem(j // 2 + nx - me, nx) + j % 2 for j in range(units)]

    def in_copy(j, slot):
        return pltpu.make_async_copy(
            xs[j], x.at[pl.ds(slot * unit_rows, unit_rows)], in_sem.at[slot]
        )

    lays = [
        pltpu.make_async_copy(
            x.at[pl.ds(slots[j] * unit_rows, unit_rows)],
            x_all.at[pl.ds(first_row + j * unit_rows, unit_rows)],
            lay_sem.at[j],
        )
        for j in range(units)
    ]
    for j in range(units):
        in_copy(j, slots[j]).start()
    rows = outs[0].shape[0]
    places = [0, rows, 3 * rows, 2 * rows, 2 * rows + rows // 2]
    group = 2 * rows
    sends = []
    for start in range(0, 4 * rows, group):
        for slot in range(start // unit_rows, (start + group) // unit_rows):
            in_copy(0, slot).wait()
        here = slice(start, start + group)
        y[here] = jnp.dot(x[here], w[...], preferred_element_type=F32).astype(BF16)
        for i, out in enumerate(outs):
            if start <= places[i] < start + group:
                src = y.at[pl.ds(places[i], out.shape[0])]
                sends.append(pltpu.make_async_copy(src, out, out_sem.at[i]))
                sends[-1].start()
    for c in lays:
        c.start()
    for c in lays + sends:
        c.wait()


def project(xs, w_vmem, seq, first_row, x_all=None, after=()):
    units, (unit_rows, depth), width = len(xs), xs[0].shape, w_vmem.shape[1]
    hbm = pl.BlockSpec(memory_space=pltpu.HBM)
    others = ([] if x_all is None else [x_all]) + list(after)
    quarter = pltpu.HBM((units * unit_rows // 4, width), BF16)
    half = pltpu.HBM((units * unit_rows // 8, width), BF16)
    xs = [pltpu.with_memory_space_constraint(v, pltpu.HBM) for v in xs]
    *parts, x_all = pl.pallas_call(
        functools.partial(project_kernel, units, unit_rows, first_row, len(others)),
        out_shape=[quarter] * 3 + [half] * 2 + [pltpu.HBM((seq, depth), BF16)],
        in_specs=[hbm] * units + [pl.BlockSpec(memory_space=pltpu.VMEM)] + [hbm] * len(others),
        out_specs=[hbm] * 6,
        scratch_shapes=[
            pltpu.VMEM((units * unit_rows, depth), BF16),
            pltpu.VMEM((units * unit_rows, width), BF16),
            pltpu.SemaphoreType.DMA((units,)),
            pltpu.SemaphoreType.DMA((units,)),
            pltpu.SemaphoreType.DMA((5,)),
        ],
        input_output_aliases={} if x_all is None else {units + 1: 5},
        compiler_params=pltpu.CompilerParams(vmem_limit_bytes=24 * 1024 * 1024),
        cost_estimate=pl.CostEstimate(
            flops=2 * units * unit_rows * depth * width,
            bytes_accessed=2 * units * unit_rows * (2 * depth + width),
            transcendentals=0,
        ),
    )(*xs, w_vmem, *others)
    return parts, x_all


def add_halves_kernel(above, below, from_below, from_above, above_out, below_out):
    first = pl.program_id(0) == 0

    @pl.when(first)
    def _():
        above_out[...] = (above[...].astype(F32) + from_below[...].astype(F32)).astype(BF16)
        below_out[...] = below[...]

    @pl.when(jnp.logical_not(first))
    def _():
        above_out[...] = above[...]
        below_out[...] = (below[...].astype(F32) + from_above[...].astype(F32)).astype(BF16)


def add_halves(above, below, from_below, from_above):
    half = pl.BlockSpec(from_below.shape, lambda i: (0, 0))
    return pl.pallas_call(
        add_halves_kernel,
        grid=(2,),
        out_shape=[jax.ShapeDtypeStruct(above.shape, BF16)] * 2,
        in_specs=[by_rows(above), by_rows(below), half, half],
        out_specs=[by_rows(above)] * 2,
    )(above, below, from_below, from_above)


def sum_beside_kernel(count, *refs):
    total = refs[0][...].astype(F32)
    for r in refs[1:count]:
        total = total + r[...].astype(F32)
    width = total.shape[1]
    out = refs[-1]
    out[:, :width] = total.astype(BF16)
    out[:, width:] = refs[count][...]


def by_rows(array, steps=2):
    rows, width = array.shape
    return pl.BlockSpec((rows // steps, width), lambda i: (i, 0))


def sum_beside(parts, beside):
    rows, width = parts[0].shape
    out = jax.ShapeDtypeStruct((rows, width + beside.shape[1]), BF16)
    return pl.pallas_call(
        functools.partial(sum_beside_kernel, len(parts)),
        grid=(2,),
        out_shape=out,
        in_specs=[by_rows(p) for p in (*parts, beside)],
        out_specs=by_rows(out),
    )(*parts, beside)


def merge_kernel(width, mine, got, out):
    total = mine[:, :width].astype(F32) + got[:, :width].astype(F32)
    out[:, :width] = total.astype(BF16)
    out[:, width : mine.shape[1]] = mine[:, width:]
    out[:, mine.shape[1] :] = got[:, width:]


def merge(mine, got, width):
    rows, both = mine.shape
    out = jax.ShapeDtypeStruct((rows, 2 * both - width), BF16)
    return pl.pallas_call(
        functools.partial(merge_kernel, width),
        grid=(2,),
        out_shape=out,
        in_specs=[by_rows(mine), by_rows(got)],
        out_specs=by_rows(out),
    )(mine, got)


def attention_kernel(heads, order, unit_rows, *refs):
    pieces, (w_hbm, att_out, grad_out) = refs[:10], refs[10:13]
    g_outs = refs[13 : 13 + len(order)]
    qkv, og, att, grad, dk_acc, dv_acc, w, in_sem, w_sem, out_sem = refs[13 + len(order) :]
    seq, width = qkv.shape
    out_rows = att_out.shape[0]
    units = len(order)
    nx = 4
    row, col = lax.axis_index("row"), lax.axis_index("col")
    x, hi = lax.rem(row, nx), lax.div(row, nx)
    nz = units // 2
    z, y_own = lax.rem(col, nz), lax.div(col, nz)
    starts = []
    for d, u in order:
        half = y_own if u == 0 else 1 - y_own
        starts.append(half * (nz * unit_rows) + lax.rem(z + d + nz, nz) * unit_rows)
    starts = [pl.multiple_of(p, unit_rows) for p in starts]
    copies = []

    def bring(src, dst):
        copies.append(pltpu.make_async_copy(src, dst, in_sem.at[len(copies)]))

    for j, piece in enumerate(pieces):
        shift, first_u = ((0, 0), (nx - 1, 0), (1, 0), (2, 0), (2, 1))[j % 5]
        sender = lax.rem(x + shift, nx)
        rows = piece.shape[0]
        for u in range(rows // unit_rows):
            first = j // 5 * (units // 2) + first_u + u
            at = starts[first]
            for q in range(1, nx):
                at = jnp.where(sender == q, starts[first + 2 * q], at)
            at = pl.multiple_of(at, unit_rows)
            src = piece.at[pl.ds(u * unit_rows, unit_rows), pl.ds(0, width)]
            bring(src, qkv.at[pl.ds(at, unit_rows)])
        if j < 5:
            for u in range(2):
                at = ((hi if u == 0 else 1 - hi) * nx + sender) * out_rows + first_u * unit_rows
                src = piece.at[:, pl.ds(width + u * heads * HD, heads * HD)]
                bring(src, og.at[pl.ds(pl.multiple_of(at, unit_rows), rows)])
    for c in copies:
        c.start()
    for c in copies:
        c.wait()
    w_copy = pltpu.make_async_copy(w_hbm, w, w_sem)
    w_copy.start()
    inv_root = 1.0 / math.sqrt(HD)
    to_base2 = inv_root * math.log2(math.e)
    nt = (((1,), (1,)), ((), ()))
    nn = (((1,), (0,)), ((), ()))
    half = QB // 2
    key_pos = lax.broadcasted_iota(jnp.int32, (half, half), 0)
    visible = key_pos <= lax.broadcasted_iota(jnp.int32, (half, half), 1)
    hidden = F32(-1e30)

    def dot(a, b, dims):
        return lax.dot_general(a, b, dims, preferred_element_type=F32)

    def join(*parts, axis=1):
        return jnp.concatenate(parts, axis=axis)

    for i in reversed(range(seq // QB)):
        rows, end = slice(i * QB, (i + 1) * QB), (i + 1) * QB
        lo = end - half
        for h in range(heads):
            base = h * 3 * HD
            k_t = qkv[:end, base + HD : base + 2 * HD].T
            v_t = qkv[:end, base + 2 * HD : base + 3 * HD].T
            q = qkv[rows, base : base + HD]
            k = qkv[:end, base + HD : base + 2 * HD]
            v = qkv[:end, base + 2 * HD : base + 3 * HD]
            g = og[rows, h * HD : (h + 1) * HD]
            s1 = dot(k[:lo], q, nt)
            s2 = jnp.where(visible, dot(k[lo:], q[half:], nt), hidden)
            edge = join(jnp.where(visible, s1[lo - half :, :half], hidden), s1[lo - half :, half:])
            s1 = edge if lo == half else join(s1[: lo - half], edge, axis=0)
            top1 = jnp.max(s1, axis=0, keepdims=True)
            top2 = jnp.max(s2, axis=0, keepdims=True)
            top = join(top1[:, :half], jnp.maximum(top1[:, half:], top2))
            e1 = jnp.exp2((s1 - top) * to_base2)
            e2 = jnp.exp2((s2 - top[:, half:]) * to_base2)
            sum1 = jnp.sum(e1, axis=0, keepdims=True)
            sum2 = jnp.sum(e2, axis=0, keepdims=True)
            inv = 1.0 / join(sum1[:, :half], sum1[:, half:] + sum2)
            p1, p2 = e1 * inv, e2 * inv[:, half:]
            b1, b2 = p1.astype(BF16), p2.astype(BF16)
            at = dot(v_t[:, :lo], b1, nn)
            at = join(at[:, :half], at[:, half:] + dot(v_t[:, lo:], b2, nn)).astype(BF16)
            dots = jnp.sum(g.T.astype(F32) * at.astype(F32), axis=0, keepdims=True)
            att[rows, h * HD : (h + 1) * HD] = at.T
            d1 = (p1 * (dot(v[:lo], g, nt) - dots)).astype(BF16)
            d2 = (p2 * (dot(v[lo:], g[half:], nt) - dots[:, half:])).astype(BF16)
            dq = dot(k_t[:, :lo], d1, nn)
            dq = join(dq[:, :half], dq[:, half:] + dot(k_t[:, lo:], d2, nn)) * inv_root
            grad[rows, base : base + HD] = dq.astype(BF16).T
            for acc, x1, x2, y in ((dk_acc, d1, d2, q), (dv_acc, b1, b2, g)):
                first, last = dot(x1, y, nn), dot(x2, y[half:], nn)
                if end == seq:
                    acc[h, :lo] = first
                    acc[h, lo:end] = last
                else:
                    acc[h, :lo] += first
                    acc[h, lo:end] += last
    for h in range(heads):
        base = h * 3 * HD
        grad[:, base + HD : base + 2 * HD] = (dk_acc[h] * inv_root).astype(BF16)
        grad[:, base + 2 * HD : base + 3 * HD] = dv_acc[h].astype(BF16)

    outs = [
        pltpu.make_async_copy(
            att.at[pl.ds(pl.multiple_of(row * out_rows, out_rows), out_rows)],
            att_out,
            out_sem.at[units],
        )
    ]
    for j in range(units):
        outs.append(
            pltpu.make_async_copy(
                grad.at[pl.ds(starts[j], unit_rows)],
                grad_out.at[pl.ds(j * unit_rows, unit_rows)],
                out_sem.at[j],
            )
        )
    for c in outs:
        c.start()
    w_copy.wait()
    tile = w.shape[0] // 2

    @pl.loop(0, 2)
    def _(n):
        cols = pl.ds(pl.multiple_of(n * tile, tile), tile)
        for first in range(0, units, 4):
            group = range(first, first + 4)
            rows = jnp.concatenate([grad[pl.ds(starts[j], unit_rows)] for j in group], axis=0)
            y = dot(rows, w[cols], nt).astype(BF16)
            for i, j in enumerate(group):
                g_outs[j][:, cols] = y[i * unit_rows : (i + 1) * unit_rows]

    for c in outs:
        c.wait()


def attention(order, unit_rows, pieces, w_qkv, own_rows):
    depth, width = w_qkv.shape
    seq = sum(p.shape[0] for p in pieces)
    units = seq // unit_rows
    heads = width // (3 * HD)
    hbm = pl.BlockSpec(memory_space=pltpu.HBM)
    vmem = pl.BlockSpec(memory_space=pltpu.VMEM)
    attended, grads, *parts = pl.pallas_call(
        functools.partial(attention_kernel, heads, order, unit_rows),
        out_shape=[
            pltpu.HBM((own_rows, heads * HD), BF16),
            pltpu.HBM((seq, width), BF16),
        ]
        + [jax.ShapeDtypeStruct((unit_rows, depth), BF16)] * units,
        in_specs=[hbm] * (len(pieces) + 1),
        out_specs=[hbm, hbm] + [vmem] * units,
        scratch_shapes=[
            pltpu.VMEM((seq, width), BF16),
            pltpu.VMEM((seq, heads * HD), BF16),
            pltpu.VMEM((seq, heads * HD), BF16),
            pltpu.VMEM((seq, width), BF16),
            pltpu.VMEM((heads, seq, HD), F32),
            pltpu.VMEM((heads, seq, HD), F32),
            pltpu.VMEM((depth, width), BF16),
            pltpu.SemaphoreType.DMA((units + len(pieces),)),
            pltpu.SemaphoreType.DMA,
            pltpu.SemaphoreType.DMA((units + 1,)),
        ],
        compiler_params=pltpu.CompilerParams(vmem_limit_bytes=50 * 1024 * 1024),
        cost_estimate=pl.CostEstimate(
            flops=12 * heads * seq * seq * HD * 5 // 8,
            bytes_accessed=2 * seq * (width * 2 + heads * HD * 2),
            transcendentals=heads * seq * seq * 5 // 8,
        ),
    )(*pieces, w_qkv)
    return attended, grads, list(parts)


def per_device(inputs, w_qkv, out_grad):
    tok = inputs.shape[0]
    own_rows = out_grad.shape[0]
    rows = lax.axis_size("row")
    cols = lax.axis_size("col")
    nz = cols // 2
    seq = cols * tok

    def along_z(step):
        return [(y * nz + a, y * nz + (a + step) % nz) for y in range(2) for a in range(nz)]

    def up(v):
        return lax.ppermute(v, "col", along_z(1))

    def down(v):
        return lax.ppermute(v, "col", along_z(-1))

    def swap_y(v):
        return lax.ppermute(v, "col", [(c, (c + nz) % cols) for c in range(cols)])

    nx = rows // 2

    def along_x(v, step):
        perm = [(y * nx + a, y * nx + (a + step) % nx) for y in range(2) for a in range(nx)]
        return lax.ppermute(v, "row", perm)

    def swap_hi(v):
        return lax.ppermute(v, "row", [(r, (r + nx) % rows) for r in range(rows)])

    def add(*parts):
        return sum(p.astype(F32) for p in parts).astype(BF16)

    def over_x(parts, *before):
        own, above, below, opposite_up, opposite_down = parts
        got = along_x(opposite_up, 1), along_x(opposite_down, nx - 1)
        *got, before = lax.optimization_barrier((*got, before))
        above, below = add_halves(above, below, *got)
        return [own, along_x(above, 1), along_x(below, nx - 1)], before

    def to_x(own):
        below, above = along_x(own, 1), along_x(own, nx - 1)
        half = own.shape[0] // 2
        opposite = [along_x(below[:half], 1), along_x(above[half:], nx - 1)]
        return [own, below, above] + opposite

    a0 = inputs
    w_vmem = hold(w_qkv)
    c0 = swap_y(inputs)
    af1, ab1 = up(a0), down(a0)
    c0, w_vmem = lax.optimization_barrier((c0, w_vmem))
    cf1, cb1 = up(c0), down(c0)
    af2, ab2 = up(af1), down(ab1)
    units = [a0, c0, af1, ab1, cf1, cb1, af2, ab2]
    parts, x_all = project(units, w_vmem, seq, 0)
    cf2, cb2 = up(cf1), down(cb1)
    af3, ab3 = up(af2), down(ab2)
    cf2, cb2, *parts = lax.optimization_barrier((cf2, cb2, *parts))
    cf3, cb3 = up(cf2), down(cb2)
    order = [(0, 0), (0, 1), (-1, 0), (1, 0), (-1, 1), (1, 1), (-2, 0), (2, 0)]
    order += [(-2, 1), (2, 1), (3, 0), (-3, 1), (-3, 0), (3, 1), (4, 0), (4, 1)]
    width = w_qkv.shape[1]
    got, (cf3, cb3) = over_x(parts, cf3, cb3)
    a4, c4 = up(af3), down(cb3)
    got[0], a4, c4 = lax.optimization_barrier((got[0], a4, c4))
    mine = sum_beside(got, out_grad)
    units = [cf2, cb2, ab3, cf3, af3, cb3, a4, c4]
    parts, x_all = project(units, w_vmem, seq, seq // 2, x_all)
    *parts, mine = lax.optimization_barrier((*parts, mine))
    other = swap_hi(mine)
    got, (other,) = over_x(parts, other)
    pieces = to_x(merge(mine, other, width))
    got[0], pieces[1], pieces[2] = lax.optimization_barrier((got[0], pieces[1], pieces[2]))
    mine = add(*got)
    pieces += to_x(add(mine, swap_hi(mine)))

    attended, grads, g = attention(order, tok, pieces, w_qkv, own_rows)
    g = dict(zip(order, g))

    c_down, a_up = down(g[4, 1]), up(g[4, 0])
    c_up, a_down = up(g[3, 1]), down(g[-3, 0])
    c_down, a_up = down(add(g[-3, 1], c_down)), up(add(g[3, 0], a_up))
    c_up, a_down = up(add(g[2, 1], c_up)), down(add(g[-2, 0], a_down))
    c_down, a_up = down(add(g[-2, 1], c_down)), up(add(g[2, 0], a_up))
    c_up, a_down = up(add(g[1, 1], c_up)), down(add(g[-1, 0], a_down))
    c_down, a_up = down(add(g[-1, 1], c_down)), up(add(g[1, 0], a_up))
    other = swap_y(add(g[0, 1], c_up, c_down))
    input_grad = add(g[0, 0], a_up, a_down, other)

    weight_grad = lax.dot_general(
        x_all, grads, (((0,), (0,)), ((), ())), preferred_element_type=F32
    ).astype(BF16)
    return attended, input_grad, weight_grad


def solution(mesh):
    placed = (P(("rep", "col"), "row"), P("row", "col"), P(("rep", "row"), "col"))
    return jax.shard_map(
        per_device,
        mesh=mesh,
        in_specs=placed,
        out_specs=(P(("rep", "row"), "col"), P(("rep", "col"), "row"), P(("rep", "row"), "col")),
        check_vma=False,
    )
```

```python
import functools
import math

import jax
import jax.numpy as jnp
from jax import lax
from jax.experimental import pallas as pl
from jax.experimental.pallas import tpu as pltpu
from jax.sharding import PartitionSpec as P

HD = 128
QB = 512
F32 = jnp.float32
BF16 = jnp.bfloat16


def hold_kernel(w_hbm, w, sem):
    step = w.shape[0] // sem.shape[0]
    copies = [
        pltpu.make_async_copy(w_hbm.at[pl.ds(i * step, step)], w.at[pl.ds(i * step, step)], sem.at[i])
        for i in range(sem.shape[0])
    ]
    for c in copies:
        c.start()
    for c in copies:
        c.wait()


def hold(w_qkv):
    return pl.pallas_call(
        hold_kernel,
        out_shape=pltpu.VMEM(w_qkv.shape, BF16),
        in_specs=[pl.BlockSpec(memory_space=pltpu.HBM)],
        out_specs=pl.BlockSpec(memory_space=pltpu.VMEM),
        scratch_shapes=[pltpu.SemaphoreType.DMA((8,))],
    )(w_qkv)


def project_kernel(units, unit_rows, first_row, others, *refs):
    xs, w = refs[:units], refs[units]
    outs, x_all = refs[units + 1 + others : -6], refs[-6]
    x, y, in_sem, lay_sem, out_sem = refs[-5:]
    nx = units // 2
    me = lax.rem(lax.axis_index("row"), nx)
    slots = [2 * lax.rem(j // 2 + nx - me, nx) + j % 2 for j in range(units)]
    slots = [pl.multiple_of(slot * unit_rows, unit_rows) for slot in slots]

    def in_copy(j):
        return pltpu.make_async_copy(xs[j], x.at[pl.ds(slots[j], unit_rows)], in_sem.at[j])

    lays = [
        pltpu.make_async_copy(
            x.at[pl.ds(slots[j], unit_rows)],
            x_all.at[pl.ds(first_row + j * unit_rows, unit_rows)],
            lay_sem.at[j],
        )
        for j in range(units)
    ]
    for j in range(units):
        in_copy(j).start()
    for j in range(units):
        in_copy(j).wait()
    for c in lays:
        c.start()
    tile = 3 * HD
    rows = outs[0].shape[0]
    places = [0, rows, 3 * rows, 2 * rows, 2 * rows + rows // 2]
    sends = []
    for n in range(w.shape[1] // tile):
        cols = slice(n * tile, (n + 1) * tile)
        y[:, cols] = jnp.dot(x[...], w[:, cols], preferred_element_type=F32).astype(BF16)
        for i, out in enumerate(outs):
            src = y.at[pl.ds(places[i], out.shape[0]), pl.ds(n * tile, tile)]
            sends.append(
                pltpu.make_async_copy(src, out.at[:, pl.ds(n * tile, tile)], out_sem.at[n, i])
            )
            sends[-1].start()
    for c in lays + sends:
        c.wait()


def project(xs, w_vmem, seq, first_row, x_all=None, after=()):
    units, (unit_rows, depth), width = len(xs), xs[0].shape, w_vmem.shape[1]
    hbm = pl.BlockSpec(memory_space=pltpu.HBM)
    others = ([] if x_all is None else [x_all]) + list(after)
    quarter = pltpu.HBM((units * unit_rows // 4, width), BF16)
    half = pltpu.HBM((units * unit_rows // 8, width), BF16)
    xs = [pltpu.with_memory_space_constraint(v, pltpu.HBM) for v in xs]
    *parts, x_all = pl.pallas_call(
        functools.partial(project_kernel, units, unit_rows, first_row, len(others)),
        out_shape=[quarter] * 3 + [half] * 2 + [pltpu.HBM((seq, depth), BF16)],
        in_specs=[hbm] * units + [pl.BlockSpec(memory_space=pltpu.VMEM)] + [hbm] * len(others),
        out_specs=[hbm] * 6,
        scratch_shapes=[
            pltpu.VMEM((units * unit_rows, depth), BF16),
            pltpu.VMEM((units * unit_rows, width), BF16),
            pltpu.SemaphoreType.DMA((units,)),
            pltpu.SemaphoreType.DMA((units,)),
            pltpu.SemaphoreType.DMA((width // (3 * HD), 5)),
        ],
        input_output_aliases={} if x_all is None else {units + 1: 5},
        compiler_params=pltpu.CompilerParams(vmem_limit_bytes=24 * 1024 * 1024),
        cost_estimate=pl.CostEstimate(
            flops=2 * units * unit_rows * depth * width,
            bytes_accessed=2 * units * unit_rows * (2 * depth + width),
            transcendentals=0,
        ),
    )(*xs, w_vmem, *others)
    return parts, x_all


def add_halves_kernel(above, below, from_below, from_above, above_out, below_out):
    first = pl.program_id(0) == 0

    @pl.when(first)
    def _():
        above_out[...] = (above[...].astype(F32) + from_below[...].astype(F32)).astype(BF16)
        below_out[...] = below[...]

    @pl.when(jnp.logical_not(first))
    def _():
        above_out[...] = above[...]
        below_out[...] = (below[...].astype(F32) + from_above[...].astype(F32)).astype(BF16)


def add_halves(above, below, from_below, from_above):
    half = pl.BlockSpec(from_below.shape, lambda i: (0, 0))
    return pl.pallas_call(
        add_halves_kernel,
        grid=(2,),
        out_shape=[jax.ShapeDtypeStruct(above.shape, BF16)] * 2,
        in_specs=[by_rows(above), by_rows(below), half, half],
        out_specs=[by_rows(above)] * 2,
    )(above, below, from_below, from_above)


def sum_beside_kernel(count, *refs):
    total = refs[0][...].astype(F32)
    for r in refs[1:count]:
        total = total + r[...].astype(F32)
    width = total.shape[1]
    out = refs[-1]
    out[:, :width] = total.astype(BF16)
    out[:, width:] = refs[count][...]


def by_rows(array, steps=2):
    rows, width = array.shape
    return pl.BlockSpec((rows // steps, width), lambda i: (i, 0))


def sum_beside(parts, beside):
    rows, width = parts[0].shape
    out = jax.ShapeDtypeStruct((rows, width + beside.shape[1]), BF16)
    return pl.pallas_call(
        functools.partial(sum_beside_kernel, len(parts)),
        grid=(2,),
        out_shape=out,
        in_specs=[by_rows(p) for p in (*parts, beside)],
        out_specs=by_rows(out),
    )(*parts, beside)


def merge_kernel(width, mine, got, out):
    total = mine[:, :width].astype(F32) + got[:, :width].astype(F32)
    out[:, :width] = total.astype(BF16)
    out[:, width : mine.shape[1]] = mine[:, width:]
    out[:, mine.shape[1] :] = got[:, width:]


def merge(mine, got, width):
    rows, both = mine.shape
    out = jax.ShapeDtypeStruct((rows, 2 * both - width), BF16)
    return pl.pallas_call(
        functools.partial(merge_kernel, width),
        grid=(2,),
        out_shape=out,
        in_specs=[by_rows(mine), by_rows(got)],
        out_specs=by_rows(out),
    )(mine, got)


def attention_kernel(heads, order, unit_rows, *refs):
    pieces, (w_hbm, att_out, grad_out) = refs[:10], refs[10:13]
    g_outs = refs[13 : 13 + len(order)]
    qkv, og, att, grad, dk_acc, dv_acc, w, in_sem, w_sem, out_sem = refs[13 + len(order) :]
    seq, width = qkv.shape
    out_rows = att_out.shape[0]
    units = len(order)
    nx = 4
    row, col = lax.axis_index("row"), lax.axis_index("col")
    x, hi = lax.rem(row, nx), lax.div(row, nx)
    nz = units // 2
    z, y_own = lax.rem(col, nz), lax.div(col, nz)
    starts = []
    for d, u in order:
        half = y_own if u == 0 else 1 - y_own
        starts.append(half * (nz * unit_rows) + lax.rem(z + d + nz, nz) * unit_rows)
    starts = [pl.multiple_of(p, unit_rows) for p in starts]
    copies = []

    def bring(src, dst):
        copies.append(pltpu.make_async_copy(src, dst, in_sem.at[len(copies)]))

    for j, piece in enumerate(pieces):
        shift, first_u = ((0, 0), (nx - 1, 0), (1, 0), (2, 0), (2, 1))[j % 5]
        sender = lax.rem(x + shift, nx)
        rows = piece.shape[0]
        for u in range(rows // unit_rows):
            first = j // 5 * (units // 2) + first_u + u
            at = starts[first]
            for q in range(1, nx):
                at = jnp.where(sender == q, starts[first + 2 * q], at)
            at = pl.multiple_of(at, unit_rows)
            src = piece.at[pl.ds(u * unit_rows, unit_rows), pl.ds(0, width)]
            bring(src, qkv.at[pl.ds(at, unit_rows)])
        if j < 5:
            for u in range(2):
                at = ((hi if u == 0 else 1 - hi) * nx + sender) * out_rows + first_u * unit_rows
                src = piece.at[:, pl.ds(width + u * heads * HD, heads * HD)]
                bring(src, og.at[pl.ds(pl.multiple_of(at, unit_rows), rows)])
    for c in copies:
        c.start()
    for c in copies:
        c.wait()
    w_copy = pltpu.make_async_copy(w_hbm, w, w_sem)
    w_copy.start()
    inv_root = 1.0 / math.sqrt(HD)
    to_base2 = inv_root * math.log2(math.e)
    nt = (((1,), (1,)), ((), ()))
    nn = (((1,), (0,)), ((), ()))
    half = QB // 2
    key_pos = lax.broadcasted_iota(jnp.int32, (half, half), 0)
    visible = key_pos <= lax.broadcasted_iota(jnp.int32, (half, half), 1)
    hidden = F32(-1e30)

    def dot(a, b, dims):
        return lax.dot_general(a, b, dims, preferred_element_type=F32)

    def join(*parts, axis=1):
        return jnp.concatenate(parts, axis=axis)

    for i in reversed(range(seq // QB)):
        rows, end = slice(i * QB, (i + 1) * QB), (i + 1) * QB
        lo = end - half
        for h in range(heads):
            base = h * 3 * HD
            k_t = qkv[:end, base + HD : base + 2 * HD].T
            v_t = qkv[:end, base + 2 * HD : base + 3 * HD].T
            q = qkv[rows, base : base + HD]
            k = qkv[:end, base + HD : base + 2 * HD]
            v = qkv[:end, base + 2 * HD : base + 3 * HD]
            g = og[rows, h * HD : (h + 1) * HD]
            s1 = dot(k[:lo], q, nt)
            s2 = jnp.where(visible, dot(k[lo:], q[half:], nt), hidden)
            edge = join(jnp.where(visible, s1[lo - half :, :half], hidden), s1[lo - half :, half:])
            s1 = edge if lo == half else join(s1[: lo - half], edge, axis=0)
            top1 = jnp.max(s1, axis=0, keepdims=True)
            top2 = jnp.max(s2, axis=0, keepdims=True)
            top = join(top1[:, :half], jnp.maximum(top1[:, half:], top2))
            e1 = jnp.exp2((s1 - top) * to_base2)
            e2 = jnp.exp2((s2 - top[:, half:]) * to_base2)
            sum1 = jnp.sum(e1, axis=0, keepdims=True)
            sum2 = jnp.sum(e2, axis=0, keepdims=True)
            inv = 1.0 / join(sum1[:, :half], sum1[:, half:] + sum2)
            p1, p2 = e1 * inv, e2 * inv[:, half:]
            b1, b2 = p1.astype(BF16), p2.astype(BF16)
            at = dot(v_t[:, :lo], b1, nn)
            at = join(at[:, :half], at[:, half:] + dot(v_t[:, lo:], b2, nn)).astype(BF16)
            dots = jnp.sum(g.T.astype(F32) * at.astype(F32), axis=0, keepdims=True)
            att[rows, h * HD : (h + 1) * HD] = at.T
            d1 = (p1 * (dot(v[:lo], g, nt) - dots)).astype(BF16)
            d2 = (p2 * (dot(v[lo:], g[half:], nt) - dots[:, half:])).astype(BF16)
            dq = dot(k_t[:, :lo], d1, nn)
            dq = join(dq[:, :half], dq[:, half:] + dot(k_t[:, lo:], d2, nn)) * inv_root
            grad[rows, base : base + HD] = dq.astype(BF16).T
            for acc, x1, x2, y in ((dk_acc, d1, d2, q), (dv_acc, b1, b2, g)):
                first, last = dot(x1, y, nn), dot(x2, y[half:], nn)
                if end == seq:
                    acc[h, :lo] = first
                    acc[h, lo:end] = last
                else:
                    acc[h, :lo] += first
                    acc[h, lo:end] += last
    for h in range(heads):
        base = h * 3 * HD
        grad[:, base + HD : base + 2 * HD] = (dk_acc[h] * inv_root).astype(BF16)
        grad[:, base + 2 * HD : base + 3 * HD] = dv_acc[h].astype(BF16)

    outs = [
        pltpu.make_async_copy(
            att.at[pl.ds(pl.multiple_of(row * out_rows, out_rows), out_rows)],
            att_out,
            out_sem.at[units],
        )
    ]
    for j in range(units):
        outs.append(
            pltpu.make_async_copy(
                grad.at[pl.ds(starts[j], unit_rows)],
                grad_out.at[pl.ds(j * unit_rows, unit_rows)],
                out_sem.at[j],
            )
        )
    for c in outs:
        c.start()
    w_copy.wait()
    tile = w.shape[0] // 2
    for first in reversed(range(0, units, 4)):
        group = range(first, first + 4)
        rows = jnp.concatenate([grad[pl.ds(starts[j], unit_rows)] for j in group], axis=0)
        for n in range(2):
            cols = slice(n * tile, (n + 1) * tile)
            y = dot(rows, w[cols], nt).astype(BF16)
            for i, j in enumerate(group):
                g_outs[j][:, cols] = y[i * unit_rows : (i + 1) * unit_rows]
    for c in outs:
        c.wait()


def attention(order, unit_rows, pieces, w_qkv, own_rows):
    depth, width = w_qkv.shape
    seq = sum(p.shape[0] for p in pieces)
    units = seq // unit_rows
    heads = width // (3 * HD)
    hbm = pl.BlockSpec(memory_space=pltpu.HBM)
    vmem = pl.BlockSpec(memory_space=pltpu.VMEM)
    attended, grads, *parts = pl.pallas_call(
        functools.partial(attention_kernel, heads, order, unit_rows),
        out_shape=[
            pltpu.HBM((own_rows, heads * HD), BF16),
            pltpu.HBM((seq, width), BF16),
        ]
        + [jax.ShapeDtypeStruct((unit_rows, depth), BF16)] * units,
        in_specs=[hbm] * (len(pieces) + 1),
        out_specs=[hbm, hbm] + [vmem] * units,
        scratch_shapes=[
            pltpu.VMEM((seq, width), BF16),
            pltpu.VMEM((seq, heads * HD), BF16),
            pltpu.VMEM((seq, heads * HD), BF16),
            pltpu.VMEM((seq, width), BF16),
            pltpu.VMEM((heads, seq, HD), F32),
            pltpu.VMEM((heads, seq, HD), F32),
            pltpu.VMEM((depth, width), BF16),
            pltpu.SemaphoreType.DMA((units + len(pieces),)),
            pltpu.SemaphoreType.DMA,
            pltpu.SemaphoreType.DMA((units + 1,)),
        ],
        compiler_params=pltpu.CompilerParams(vmem_limit_bytes=50 * 1024 * 1024),
        cost_estimate=pl.CostEstimate(
            flops=12 * heads * seq * seq * HD * 5 // 8,
            bytes_accessed=2 * seq * (width * 2 + heads * HD * 2),
            transcendentals=heads * seq * seq * 5 // 8,
        ),
    )(*pieces, w_qkv)
    return attended, grads, list(parts)


def per_device(inputs, w_qkv, out_grad):
    tok = inputs.shape[0]
    own_rows = out_grad.shape[0]
    rows = lax.axis_size("row")
    cols = lax.axis_size("col")
    nz = cols // 2
    seq = cols * tok

    def along_z(step):
        return [(y * nz + a, y * nz + (a + step) % nz) for y in range(2) for a in range(nz)]

    def up(v):
        return lax.ppermute(v, "col", along_z(1))

    def down(v):
        return lax.ppermute(v, "col", along_z(-1))

    def swap_y(v):
        return lax.ppermute(v, "col", [(c, (c + nz) % cols) for c in range(cols)])

    nx = rows // 2

    def along_x(v, step):
        perm = [(y * nx + a, y * nx + (a + step) % nx) for y in range(2) for a in range(nx)]
        return lax.ppermute(v, "row", perm)

    def swap_hi(v):
        return lax.ppermute(v, "row", [(r, (r + nx) % rows) for r in range(rows)])

    def add(*parts):
        return sum(p.astype(F32) for p in parts).astype(BF16)

    def over_x(parts, *before, ring=False):
        own, above, below, opposite_up, opposite_down = parts
        got = along_x(opposite_up, 1), along_x(opposite_down, nx - 1)
        *got, before = lax.optimization_barrier((*got, before))
        above, below = add_halves(above, below, *got)
        if not ring:
            *before, above, below = lax.optimization_barrier((*before, above, below))
        return [own, along_x(above, 1), along_x(below, nx - 1)], before

    def to_x(own):
        below, above = along_x(own, 1), along_x(own, nx - 1)
        half = own.shape[0] // 2
        opposite = [along_x(below[:half], 1), along_x(above[half:], nx - 1)]
        return [own, below, above] + opposite

    a0 = inputs
    w_vmem = hold(w_qkv)
    c0 = swap_y(inputs)
    af1, ab1 = up(a0), down(a0)
    c0, w_vmem = lax.optimization_barrier((c0, w_vmem))
    cf1, cb1 = up(c0), down(c0)
    af2, ab2 = up(af1), down(ab1)
    units = [a0, c0, af1, ab1, cf1, cb1, af2, ab2]
    parts, x_all = project(units, w_vmem, seq, 0)
    cf2, cb2 = up(cf1), down(cb1)
    af3, ab3 = up(af2), down(ab2)
    cf2, cb2, *parts = lax.optimization_barrier((cf2, cb2, *parts))
    cf3, cb3 = up(cf2), down(cb2)
    order = [(0, 0), (0, 1), (-1, 0), (1, 0), (-1, 1), (1, 1), (-2, 0), (2, 0)]
    order += [(-2, 1), (2, 1), (3, 0), (-3, 1), (-3, 0), (3, 1), (4, 0), (4, 1)]
    width = w_qkv.shape[1]
    got, (cf3, cb3) = over_x(parts, cf3, cb3, ring=True)
    a4, c4 = up(af3), down(cb3)
    got[0], a4, c4 = lax.optimization_barrier((got[0], a4, c4))
    mine = sum_beside(got, out_grad)
    units = [cf2, cb2, ab3, cf3, af3, cb3, a4, c4]
    parts, x_all = project(units, w_vmem, seq, seq // 2, x_all)
    *parts, mine = lax.optimization_barrier((*parts, mine))
    got, (other,) = over_x(parts, swap_hi(mine))
    pieces = to_x(merge(mine, other, width))
    mine = add(*got)
    other, pieces[1], pieces[2] = lax.optimization_barrier((swap_hi(mine), pieces[1], pieces[2]))
    pieces += to_x(add(mine, other))

    attended, grads, g = attention(order, tok, pieces, w_qkv, own_rows)
    g = dict(zip(order, g))

    c_down, a_up = down(g[4, 1]), up(g[4, 0])
    c_up, a_down = up(g[3, 1]), down(g[-3, 0])
    c_down, a_up = down(add(g[-3, 1], c_down)), up(add(g[3, 0], a_up))
    c_up, a_down = up(add(g[2, 1], c_up)), down(add(g[-2, 0], a_down))
    c_down, a_up = down(add(g[-2, 1], c_down)), up(add(g[2, 0], a_up))
    c_up, a_down = up(add(g[1, 1], c_up)), down(add(g[-1, 0], a_down))
    c_down, a_up = down(add(g[-1, 1], c_down)), up(add(g[1, 0], a_up))
    other = swap_y(add(g[0, 1], c_up, c_down))
    input_grad = add(g[0, 0], a_up, a_down, other)

    weight_grad = lax.dot_general(
        x_all, grads, (((0,), (0,)), ((), ())), preferred_element_type=F32
    ).astype(BF16)
    return attended, input_grad, weight_grad


def solution(mesh):
    placed = (P(("rep", "col"), "row"), P("row", "col"), P(("rep", "row"), "col"))
    return jax.shard_map(
        per_device,
        mesh=mesh,
        in_specs=placed,
        out_specs=(P(("rep", "row"), "col"), P(("rep", "col"), "row"), P(("rep", "row"), "col")),
        check_vma=False,
    )
```
